32 devices in a mesh: slab: 8 (over y, x, core), sub: 4 (over z).
Axes of the slice: x: 2, y: 2, z: 4, core: 2. Of those that a mesh axis runs over, the one named last changes fastest.
Arguments:
- cav_disp: float32 [3, 512, 128, 128], P(None, 'slab', 'sub'), may hold values from -2 to 2
- cav_load: float32 [3, 512, 128, 128], P(None, 'slab', 'sub'), may hold values from -6 to 6
- cav_stiff: float32 [512, 128, 128], P('slab', 'sub'), may hold values from 0.5 to 4
- cav_clamp: int32 [512, 128, 128], P('slab', 'sub'), may hold values 0 or 1
- mnt_disp: float32 [3, 512, 128, 128], P(None, 'slab', 'sub'), may hold values from -2 to 2
- mnt_load: float32 [3, 512, 128, 128], P(None, 'slab', 'sub'), may hold values from -6 to 6
- mnt_stiff: float32 [512, 128, 128], P('slab', 'sub'), may hold values from 0.5 to 4
- mnt_clamp: int32 [512, 128, 128], P('slab', 'sub'), may hold values 0 or 1
- pair_owner: int32 [65536, 1], P(('slab', 'sub')), may hold values from 0 to 31, as said below
- pair_row: int32 [65536], P(('slab', 'sub')), may hold values from 0 to 2047
- pair_seg: int32 [65536], P(('slab', 'sub')), may hold values from 0 to 2047
- pair_weight: float32 [65536], P(('slab', 'sub')), may hold values from 0.2 to 2
- pair_tilt: float32 [2, 65536], P(None, ('slab', 'sub')), may hold values from -0.5 to 0.5
- pair_gap: float32 [65536], P(('slab', 'sub')), may hold values from -3 to 3
Outputs:
- cav_new: float32 [3, 512, 128, 128], P(None, 'slab', 'sub')
- mnt_new: float32 [3, 512, 128, 128], P(None, 'slab', 'sub')
The draws below stay inside these ranges and needn't reach their ends.
Inputs may be any that keep to these rules, and one draw needn't show every extreme that they name: `pair_owner`: the owner of a pair lies in the holder's slab or in the next slab along the long axis. Among the pairs of one device, at most 512 name one owner, and some owner is named exactly 512 times.
All inputs are finite; a program needn't handle non-finite values. No bound on the sum of `cav_clamp` or of `mnt_clamp` on one device may be relied on, other than what follows from the above.
Results may differ from the reference program's by a relative error of at most 0.00002.
Values sent between devices are 32-bit elements; how exact they have to be, the bound alone decides.
A program may use at most 128 MiB of HBM per device.

```python
import math
import jax
import jax.numpy as jnp
from jax import lax

CX = 64
CY = 32
CZ = 128
PAIR_DEV = 2048
NX = 512
NY = 128
PAIRS = 65536
CAP = 512
N_SLAB = 8
N_SUB = 4
DEVICES = 32


def draw_pair_owner(key, part):
    key = jax.random.fold_in(key, 11)
    first_key, second_key = jax.random.split(key)
    device = jnp.arange(DEVICES, dtype=jnp.int32)
    slab_of = device // N_SUB
    candidate = jnp.arange(2 * N_SUB, dtype=jnp.int32)
    cand_slab = slab_of[:, None] + candidate[None, :] // N_SUB
    cand_device = cand_slab * N_SUB + candidate[None, :] % N_SUB
    usable = cand_slab < N_SLAB
    scores = jax.random.randint(first_key, (DEVICES, 2 * N_SUB), 0, 65536) * (2 * N_SUB) + candidate[None, :]
    scores = jnp.where(usable, scores, -1)
    ordering = jnp.argsort(-scores, axis=1)
    usable_count = jnp.sum(usable.astype(jnp.int32), axis=1)
    position = jnp.arange(PAIR_DEV, dtype=jnp.int32)
    picked = jnp.where(position[None, :] < CAP, 0, 1 + (position[None, :] - CAP) % (usable_count[:, None] - 1))
    chosen = jnp.take_along_axis(ordering, picked, axis=1)
    owners = jnp.take_along_axis(cand_device, chosen, axis=1)
    owners = jax.random.permutation(second_key, owners, axis=1, independent=True)
    return owners.reshape(PAIRS, 1).astype(jnp.int32)


def set_ends(drawn, stream_key, low, largest):
    shape = drawn.shape
    spot = [jax.random.randint(jax.random.fold_in(stream_key, axis), (), 0, shape[axis]) for axis in range(len(shape))]
    drawn = drawn.at[tuple(spot)].set(low)
    longest = shape.index(max(shape))
    spot[longest] = (spot[longest] + 1) % shape[longest]
    return drawn.at[tuple(spot)].set(largest)


def steps_of(rng, shape, cuts, low, high):
    def one(axis_at, shards_of):
        draws = jax.random.uniform(jax.random.fold_in(jax.random.fold_in(rng, 6), axis_at), (shards_of,), jnp.float32, low / len(cuts), high / len(cuts))
        return jnp.repeat(jnp.exp(draws), shape[axis_at] // shards_of).reshape((-1,) + (1,) * (len(shape) - axis_at - 1))

    gain = one(*cuts[0])
    for cut in cuts[1:]:
        gain = gain * one(*cut)
    return gain


def centred(own_key, dims, scale, bound, pieces=(), held_as=jnp.bfloat16):
    entries = scale * jax.random.normal(own_key, dims, jnp.float32)
    if pieces:
        entries = entries * steps_of(own_key, dims, pieces, -0.22, 0.18)
    return jnp.clip(entries, -bound, bound).astype(held_as)


def setup_inputs(seed: int = 0) -> dict:
    keys = jax.random.split(jax.random.key(seed), 15)
    cav_disp = centred(keys[0], (3, NX, NY, CZ), 0.3, 2.0, ((1, 8), (2, 4)), jnp.float32)
    cav_load = centred(keys[1], (3, NX, NY, CZ), 1.0, 6.0, ((1, 8), (2, 4)), jnp.float32)
    cav_stiff = jnp.clip(jnp.exp(math.log(4.0) - 2.0794415 * jax.random.uniform(keys[2], (NX, NY, CZ), jnp.float32) ** steps_of(keys[2], (NX, NY, CZ), ((0, 8), (1, 4)), -0.2, 0.2)), 0.5, 4.0)
    cav_clamp = set_ends((jax.random.randint(keys[3], (NX, NY, CZ), 0, 8) < 1).astype(jnp.int32), jax.random.fold_in(keys[3], 1), 0, 1)
    mnt_disp = centred(keys[4], (3, NX, NY, CZ), 0.3, 2.0, ((1, 8), (2, 4)), jnp.float32)
    mnt_load = centred(keys[5], (3, NX, NY, CZ), 1.0, 6.0, ((1, 8), (2, 4)), jnp.float32)
    mnt_stiff = jnp.clip(jnp.exp(math.log(4.0) - 2.0794415 * jax.random.uniform(keys[6], (NX, NY, CZ), jnp.float32) ** steps_of(keys[6], (NX, NY, CZ), ((0, 8), (1, 4)), -0.2, 0.2)), 0.5, 4.0)
    mnt_clamp = set_ends((jax.random.randint(keys[7], (NX, NY, CZ), 0, 8) < 1).astype(jnp.int32), jax.random.fold_in(keys[7], 1), 0, 1)
    pair_owner = draw_pair_owner(jax.random.fold_in(keys[14], 71), 0)
    pair_row = set_ends(jax.random.randint(keys[9], (PAIRS,), 0, CX * CY), jax.random.fold_in(keys[9], 1), 0, (CX * CY) - 1).astype(jnp.int32)
    pair_seg = set_ends(jax.random.randint(keys[10], (PAIRS,), 0, CX * CY), jax.random.fold_in(keys[10], 1), 0, (CX * CY) - 1).astype(jnp.int32)
    pair_weight = jnp.clip(jnp.exp(math.log(2.0) - 2.3025851 * jax.random.uniform(keys[11], (PAIRS,), jnp.float32) ** steps_of(keys[11], (PAIRS,), ((0, 32),), -0.2, 0.2)), 0.2, 2.0)
    pair_tilt = jnp.clip(jax.random.uniform(keys[12], (2, PAIRS), jnp.float32, -0.5, 0.5) * steps_of(keys[12], (2, PAIRS), ((1, 32),), -0.4, 0.0), -0.5, 0.5)
    pair_gap = centred(keys[13], (PAIRS,), 0.5, 3.0, ((0, 32),), jnp.float32)
    return {"cav_disp": cav_disp, "cav_load": cav_load, "cav_stiff": cav_stiff, "cav_clamp": cav_clamp, "mnt_disp": mnt_disp, "mnt_load": mnt_load, "mnt_stiff": mnt_stiff, "mnt_clamp": mnt_clamp, "pair_owner": pair_owner, "pair_row": pair_row, "pair_seg": pair_seg, "pair_weight": pair_weight, "pair_tilt": pair_tilt, "pair_gap": pair_gap}


OMEGA = 0.8
KCLAMP = 4.0
KNORM = 2.0
BETA = 4.0

def relax(disp, force, stiff, clamp):
    held = clamp.astype(jnp.float32)
    diag = 6.0 * stiff + KCLAMP * held
    for step in range(2):
        padded = jnp.pad(disp, ((0, 0), (1, 1), (1, 1), (1, 1)))
        beside = padded[:, 2:, 1:-1, 1:-1] + padded[:, :-2, 1:-1, 1:-1]
        beside = beside + padded[:, 1:-1, 2:, 1:-1] + padded[:, 1:-1, :-2, 1:-1]
        beside = beside + padded[:, 1:-1, 1:-1, 2:] + padded[:, 1:-1, 1:-1, :-2]
        applied = stiff * (6.0 * disp - beside) + KCLAMP * held * disp
        disp = disp + OMEGA * (force - applied) / diag
    return disp

def reference(cav_disp, cav_load, cav_stiff, cav_clamp, mnt_disp, mnt_load, mnt_stiff, mnt_clamp, pair_owner, pair_row, pair_seg, pair_weight, pair_tilt, pair_gap):
    holder = jnp.arange(PAIRS, dtype=jnp.int32) // PAIR_DEV
    cav_x = holder // N_SUB * CX + pair_row // CY
    cav_y = holder % N_SUB * CY + pair_row % CY
    owner = pair_owner[:, 0]
    mnt_x = owner // N_SUB * CX + pair_seg // CY
    mnt_y = owner % N_SUB * CY + pair_seg % CY
    slope_a = pair_tilt[0]
    slope_b = pair_tilt[1]
    scale = 1.0 / jnp.sqrt(1.0 + slope_a * slope_a + slope_b * slope_b)
    normal = jnp.stack([slope_a * scale, slope_b * scale, scale])
    cav_side = cav_disp[:, cav_x, cav_y, CZ - 1]
    mnt_side = mnt_disp[:, mnt_x, mnt_y, 0]
    gap = pair_gap + lax.optimization_barrier(jnp.sum(normal * (cav_side - mnt_side), axis=0))
    press = pair_weight * (KNORM * jax.nn.softplus(-BETA * gap) / BETA)
    push = press[None, :] * normal
    cav_force = cav_load.at[:, cav_x, cav_y, CZ - 1].add(push)
    mnt_force = mnt_load.at[:, mnt_x, mnt_y, 0].add(-push)
    cav_new = relax(cav_disp, cav_force, cav_stiff, cav_clamp)
    mnt_new = relax(mnt_disp, mnt_force, mnt_stiff, mnt_clamp)
    return (cav_new, mnt_new)
```

```python
import functools
import jax
import jax.numpy as jnp
from jax import lax
from jax.experimental import pallas as pl
from jax.experimental.pallas import tpu as pltpu
from jax.sharding import PartitionSpec as P

OMEGA = 0.8
KCLAMP = 4.0
KNORM = 2.0
BETA = 4.0
MESH = pl.DeviceIdType.MESH
F32 = jnp.float32
BF16 = jnp.bfloat16
CHUNK = 256


def split3(v):
    hi = v.astype(BF16).astype(F32)
    rest = v - hi
    mid = rest.astype(BF16).astype(F32)
    return hi, mid, rest - mid


def beside_z(v):
    axis = v.ndim - 1
    depth = v.shape[axis]
    lane = lax.broadcasted_iota(jnp.int32, v.shape, axis)
    up = jnp.where(lane == 0, 0.0, pltpu.roll(v, 1, axis))
    down = jnp.where(lane == depth - 1, 0.0, pltpu.roll(v, depth - 1, axis))
    return up + down


def beside_rows(v, before, after):
    rows = v.shape[0]
    at = lax.broadcasted_iota(jnp.int32, v.shape, 0)
    up = jnp.where(at == 0, before, pltpu.roll(v, 1, 0))
    down = jnp.where(at == rows - 1, after, pltpu.roll(v, rows - 1, 0))
    return up + down


def coefficients(stiff, clamp):
    gain = OMEGA / (6.0 * stiff + KCLAMP * clamp.astype(F32))
    return gain, gain * stiff


def contact_kernel(
    n_slab, n_sub, nx, ny,
    disp_c, disp_m, load_c, load_m, stiff_c, stiff_m, clamp_c, clamp_m,
    seg, row, own, weight, gap0, tilt,
    react, xh0, yh0, xh1, yh1,
    u, ld, st, cl, tab, part, rec, yf, xs1, ys1,
    tab_s, tab_r, part_s, part_r, h0_s, h0_r, h1_s, h1_r, in_sem,
):
    s = lax.axis_index("slab")
    t = lax.axis_index("sub")
    depth = 128
    cells = nx * ny
    half = ny // 2
    dense = 3 * half
    pairs = seg.shape[0] * 128
    has_prev = s > 0
    has_next = s < n_slab - 1
    lane_of = (depth - 1, 0)

    loads = []
    for i, (src, dst) in enumerate((
        (disp_m, u.at[1]), (disp_c, u.at[0]),
        (stiff_m, st.at[1]), (clamp_m, cl.at[1]), (load_m, ld.at[1]),
        (stiff_c, st.at[0]), (clamp_c, cl.at[0]), (load_c, ld.at[0]),
    )):
        copy = pltpu.make_async_copy(src, dst, in_sem.at[i])
        copy.start()
        loads.append(copy)

    def peer(ds, d):
        return {"slab": s + ds, "sub": lax.rem(t + d, n_sub)}

    barrier = pltpu.get_barrier_semaphore()
    for d in range(1, n_sub):
        pl.semaphore_signal(barrier, inc=1, device_id=peer(0, d), device_id_type=MESH)

    @pl.when(has_prev)
    def _():
        for d in range(n_sub):
            pl.semaphore_signal(barrier, inc=1, device_id=peer(-1, d), device_id_type=MESH)

    @pl.when(has_next)
    def _():
        for d in range(n_sub):
            pl.semaphore_signal(barrier, inc=1, device_id=peer(1, d), device_id_type=MESH)

    def densify(b):
        zc = lane_of[b]
        lane = lax.broadcasted_iota(jnp.int32, (half, depth), 1)

        def at_x(x, acc):
            acc = list(acc)
            for c in range(3):
                for h in range(2):
                    want = x + nx * h
                    start = pl.multiple_of(c * cells + x * ny + half * h, 8)
                    tile = u[b, pl.ds(start, half), :]
                    moved = pltpu.roll(tile, lax.rem(want - zc + depth, depth), 1)
                    acc[c] = jnp.where(lane == want, moved, acc[c])
            return tuple(acc)

        zero = jnp.zeros((half, depth), F32)
        return jnp.concatenate(lax.fori_loop(0, nx, at_x, (zero,) * 3, unroll=4), axis=0)

    loads[0].wait()
    tab[t] = densify(1)
    for b, side in ((1, 0), (1, 1)):
        for c in range(3):
            yf[b, side, c] = u[b, pl.ds(c * cells + side * (ny - 1), nx, stride=ny), :]

    sides = has_prev.astype(jnp.int32) + has_next.astype(jnp.int32)
    pl.semaphore_wait(barrier, n_sub - 1 + n_sub * sides)

    def remote(src, dst, ss, rs, dev):
        return pltpu.make_async_remote_copy(
            src_ref=src, dst_ref=dst, send_sem=ss, recv_sem=rs, device_id=dev, device_id_type=MESH
        )

    def tab_copy(ds, d):
        k = d if ds == 0 else n_sub + d
        slot = t if ds == 0 else n_sub + t
        return remote(tab.at[t], tab.at[slot], tab_s.at[k], tab_r.at[slot], peer(ds, d))

    def tab_arrival(ds, d):
        slot = lax.rem(t + d, n_sub) + (n_sub if ds else 0)
        return remote(tab.at[t], tab.at[slot], tab_s.at[0], tab_r.at[slot], peer(ds, d))

    for d in range(1, n_sub):
        tab_copy(0, d).start()

    @pl.when(has_prev)
    def _():
        for d in range(n_sub):
            tab_copy(-1, d).start()

    @pl.when(jnp.logical_not(has_next))
    def _():
        tab[pl.ds(n_sub, n_sub)] = jnp.zeros((n_sub, dense, depth), F32)

    def ways():
        return (
            (0, has_prev, {"slab": s - 1, "sub": t}),
            (1, has_next, {"slab": s + 1, "sub": t}),
            (2, t > 0, {"slab": s, "sub": t - 1}),
            (3, t < n_sub - 1, {"slab": s, "sub": t + 1}),
        )

    def halo_copy(b, way, dev, xsrc, ysrc, xdst, ydst, ss, rs):
        other = way ^ 1
        if way < 2:
            src, dst = xsrc(b, way), xdst.at[b, other]
        else:
            src, dst = ysrc.at[b, way - 2], ydst.at[b, other - 2]
        return remote(src, dst, ss.at[b, way], rs.at[b, other], dev)

    def halo_arrival(b, way, dev, xdst, ydst, ss, rs):
        dst = xdst.at[b, way] if way < 2 else ydst.at[b, way - 2]
        return remote(dst, dst, ss.at[b, way], rs.at[b, way], dev)

    def x_plane(b, way):
        return u.at[b].reshape(3, nx, ny, depth).at[:, (nx - 1) * way]

    def start_halo0(b):
        for way, there, dev in ways():
            @pl.when(there)
            def _():
                halo_copy(b, way, dev, x_plane, yf, xh0, yh0, h0_s, h0_r).start()

            @pl.when(jnp.logical_not(there))
            def _():
                for out_x, out_y in ((xh0, yh0), (xh1, yh1)):
                    if way < 2:
                        out_x[b, way] = jnp.zeros((3, ny, depth), F32)
                    else:
                        out_y[b, way - 2] = jnp.zeros((3, nx, depth), F32)

    start_halo0(1)
    loads[1].wait()
    for side in range(2):
        for c in range(3):
            yf[0, side, c] = u[0, pl.ds(c * cells + side * (ny - 1), nx, stride=ny), :]
    start_halo0(0)
    cav_dense = densify(0)
    cav_parts = jnp.concatenate([v.astype(BF16) for v in split3(cav_dense)], axis=1)

    for d in range(1, n_sub):
        tab_arrival(0, d).wait_recv()

    @pl.when(has_next)
    def _():
        for d in range(n_sub):
            tab_arrival(1, d).wait_recv()

    targets = 2 * n_sub
    table = tab[...].reshape(targets * dense, depth)
    tab_parts = jnp.concatenate([v.astype(BF16) for v in split3(table)], axis=1)

    def line(ref, k):
        per = CHUNK // 128
        return jnp.concatenate([ref[k * per + i : k * per + i + 1, :] for i in range(per)], axis=1)

    dot = functools.partial(
        lax.dot_general, preferred_element_type=F32, precision=lax.Precision.DEFAULT
    )
    mnt_sum = jnp.zeros((targets * dense, depth), F32)
    cav_sum = jnp.zeros((dense, depth), F32)
    lane_id = lax.broadcasted_iota(jnp.int32, (depth, CHUNK), 0)
    key_id = lax.broadcasted_iota(jnp.int32, (targets * half, CHUNK), 0)
    small_id = lax.broadcasted_iota(jnp.int32, (half, CHUNK), 0)
    for k in range(pairs // CHUNK):
        def lanes(cell):
            return cell // ny + nx * (cell % ny // half)

        seg_k, row_k = line(seg, k), line(row, k)
        target = line(own, k) - s * n_sub
        hot_m = (lane_id == lanes(seg_k)).astype(F32).astype(BF16)
        hot_c = (lane_id == lanes(row_k)).astype(F32).astype(BF16)
        mask_m = key_id == target * half + seg_k % half
        mask_c = small_id == row_k % half
        rows_m = dot(tab_parts, jnp.concatenate([hot_m] * 3, axis=0), (((1,), (0,)), ((), ())))
        rows_c = dot(cav_parts, jnp.concatenate([hot_c] * 3, axis=0), (((1,), (0,)), ((), ())))
        sl_a = tilt[0:1, k * CHUNK : (k + 1) * CHUNK]
        sl_b = tilt[1:2, k * CHUNK : (k + 1) * CHUNK]
        scale = 1.0 / jnp.sqrt(1.0 + sl_a * sl_a + sl_b * sl_b)
        normal = (sl_a * scale, sl_b * scale, scale)
        gap = line(gap0, k)
        for c in range(3):
            mine = jnp.concatenate(
                [rows_m[o * dense + c * half : o * dense + (c + 1) * half] for o in range(targets)], axis=0
            )
            side_m = jnp.sum(jnp.where(mask_m, mine, 0.0), axis=0, keepdims=True)
            side_c = jnp.sum(
                jnp.where(mask_c, rows_c[c * half : (c + 1) * half], 0.0), axis=0, keepdims=True
            )
            gap = gap + normal[c] * (side_c - side_m)
        z = -BETA * gap
        soft = jnp.maximum(z, 0.0) + jnp.log1p(jnp.exp(-jnp.abs(z)))
        press = line(weight, k) * (KNORM * soft / BETA)
        push = [split3(press * normal[c]) for c in range(3)]
        left_m, left_c = [], []
        for p in range(3):
            left_m.append(jnp.concatenate(
                [
                    jnp.where(mask_m[o * half : (o + 1) * half], push[c][p], 0.0)
                    for o in range(targets) for c in range(3)
                ], axis=0).astype(BF16))
            left_c.append(jnp.concatenate(
                [jnp.where(mask_c, push[c][p], 0.0) for c in range(3)], axis=0).astype(BF16))
        mnt_sum = mnt_sum + dot(
            jnp.concatenate(left_m, axis=1), jnp.concatenate([hot_m] * 3, axis=1), (((1,), (1,)), ((), ())))
        cav_sum = cav_sum + dot(
            jnp.concatenate(left_c, axis=1), jnp.concatenate([hot_c] * 3, axis=1), (((1,), (1,)), ((), ())))
    part[...] = mnt_sum.reshape(targets, dense, depth)
    react[0] = cav_sum

    def part_copy(ds, d):
        k = d if ds == 0 else n_sub + d
        slot = t if ds == 0 else n_sub + t
        block = lax.rem(t + d, n_sub) + (n_sub if ds else 0)
        return remote(part.at[block], rec.at[slot], part_s.at[k], part_r.at[slot], peer(ds, d))

    def part_arrival(ds, d):
        slot = lax.rem(t + d, n_sub) + (n_sub if ds else 0)
        return remote(part.at[t], rec.at[slot], part_s.at[0], part_r.at[slot], peer(ds, d))

    @pl.when(has_next)
    def _():
        for d in range(n_sub):
            part_copy(1, d).start()

    for d in range(1, n_sub):
        part_copy(0, d).start()
    rec[t] = part[t]

    @pl.when(jnp.logical_not(has_prev))
    def _():
        rec[pl.ds(n_sub, n_sub)] = jnp.zeros((n_sub, dense, depth), F32)

    for copy in loads[2:]:
        copy.wait()
    for b in range(2):
        for way, there, dev in ways():
            @pl.when(there)
            def _():
                halo_arrival(b, way, dev, xh0, yh0, h0_s, h0_r).wait_recv()

    def faces(b):
        zc = lane_of[b]
        force_b = react[b]
        turned = jnp.transpose(jnp.concatenate(
            [force_b, jnp.zeros((depth - dense, depth), F32)], axis=0))
        for side in range(2):
            x0 = side * (nx - 1)
            at_x = pl.ds(x0 * ny, ny)
            gain, pull = coefficients(st[b, at_x, :], cl[b, at_x, :])
            lane = lax.broadcasted_iota(jnp.int32, (ny, depth), 1)
            for c in range(3):
                v = u[b, pl.ds(c * cells + x0 * ny, ny), :]
                inner = u[b, pl.ds(c * cells + (x0 + 1 - 2 * side) * ny, ny), :]
                near = xh0[b, side, c] + inner + beside_z(v)
                near = near + beside_rows(v, yh0[b, 0, c, x0 : x0 + 1], yh0[b, 1, c, x0 : x0 + 1])
                rows = force_b[c * half : (c + 1) * half]
                extra = jnp.concatenate(
                    [pltpu.roll(rows, (zc - x0 - nx * h) % depth, 1) for h in range(2)], axis=0)
                force = ld[b, pl.ds(c * cells + x0 * ny, ny), :] + jnp.where(lane == zc, extra, 0.0)
                xs1[b, side, c] = (1.0 - OMEGA) * v + (gain * force + pull * near)
            y0 = side * (ny - 1)
            at_y = pl.ds(y0, nx, stride=ny)
            gain, pull = coefficients(st[b, at_y, :], cl[b, at_y, :])
            lane = lax.broadcasted_iota(jnp.int32, (nx, depth), 1)
            for c in range(3):
                v = yf[b, side, c]
                inner = u[b, pl.ds(c * cells + y0 + 1 - 2 * side, nx, stride=ny), :]
                near = yh0[b, side, c] + inner + beside_z(v)
                near = near + beside_rows(v, xh0[b, 0, c, y0 : y0 + 1], xh0[b, 1, c, y0 : y0 + 1])
                rows = turned[nx * side : nx * side + nx]
                extra = pltpu.roll(rows, (zc - c * half - y0 % half) % depth, 1)
                force = ld[b, pl.ds(c * cells + y0, nx, stride=ny), :] + jnp.where(lane == zc, extra, 0.0)
                ys1[b, side, c] = (1.0 - OMEGA) * v + (gain * force + pull * near)
        for way, there, dev in ways():
            @pl.when(there)
            def _():
                halo_copy(b, way, dev, lambda b, w: xs1.at[b, w], ys1, xh1, yh1, h1_s, h1_r).start()

    faces(0)
    for d in range(1, n_sub):
        part_arrival(0, d).wait_recv()

    @pl.when(has_prev)
    def _():
        for d in range(n_sub):
            part_arrival(-1, d).wait_recv()

    total = rec[0]
    for o in range(1, targets):
        total = total + rec[o]
    react[1] = -total
    faces(1)

    for d in range(1, n_sub):
        tab_copy(0, d).wait_send()
        part_copy(0, d).wait_send()

    @pl.when(has_prev)
    def _():
        for d in range(n_sub):
            tab_copy(-1, d).wait_send()

    @pl.when(has_next)
    def _():
        for d in range(n_sub):
            part_copy(1, d).wait_send()

    for b in range(2):
        for way, there, dev in ways():
            @pl.when(there)
            def _():
                halo_copy(b, way, dev, x_plane, yf, xh0, yh0, h0_s, h0_r).wait_send()
                halo_copy(b, way, dev, lambda b, w: xs1.at[b, w], ys1, xh1, yh1, h1_s, h1_r).wait_send()
                halo_arrival(b, way, dev, xh1, yh1, h1_s, h1_r).wait_recv()


def relax_kernel(
    nx, ny, chunks,
    disp_c, disp_m, load_c, load_m, stiff_c, stiff_m, clamp_c, clamp_m,
    react, xh0, yh0, xh1, yh1,
    out_c, out_m,
    u, w, ld, st, cl, in_sem, out_sem,
):
    depth = 128
    half = ny // 2
    step = nx // chunks
    sources = ((disp_c, load_c, stiff_c, clamp_c), (disp_m, load_m, stiff_m, clamp_m))
    outs = (out_c, out_m)

    def arrivals(b, k):
        span = pl.ds(k * step, step)
        shifted = pl.ds(k * step + 1, step)
        disp, load, stiff, clamp = sources[b]
        return (
            pltpu.make_async_copy(disp.at[:, span], u.at[b, :, shifted], in_sem.at[b, k, 0]),
            pltpu.make_async_copy(load.at[:, span], ld.at[b, :, span], in_sem.at[b, k, 1]),
            pltpu.make_async_copy(stiff.at[span], st.at[b, span], in_sem.at[b, k, 2]),
            pltpu.make_async_copy(clamp.at[span], cl.at[b, span], in_sem.at[b, k, 3]),
        )

    for b in range(2):
        for k in range(chunks):
            for copy in arrivals(b, k):
                copy.start()

    lane = lax.broadcasted_iota(jnp.int32, (ny, depth), 1)

    def first(b, k):
        zc = (depth - 1, 0)[b]

        def at_x(x, carry):
            gain, pull = coefficients(st[b, x], cl[b, x])
            st[b, x] = pull
            for c in range(3):
                v = u[b, c, x + 1]
                near = u[b, c, x] + u[b, c, x + 2] + beside_z(v)
                near = near + beside_rows(v, yh0[b, 0, c, pl.ds(x, 1)], yh0[b, 1, c, pl.ds(x, 1)])
                rows = react[b, c * half : (c + 1) * half]
                extra = jnp.concatenate(
                    [pltpu.roll(rows, lax.rem(zc - x - nx * h + 2 * depth, depth), 1) for h in range(2)], axis=0)
                push = gain * (ld[b, c, x] + jnp.where(lane == zc, extra, 0.0))
                ld[b, c, x] = push
                w[b, c, x + 1] = (1.0 - OMEGA) * v + (push + pull * near)
            return carry

        lax.fori_loop(k * step, (k + 1) * step, at_x, 0, unroll=2)

    def second(b, k):
        def at_x(x, carry):
            pull = st[b, x]
            for c in range(3):
                v = w[b, c, x + 1]
                near = w[b, c, x] + w[b, c, x + 2] + beside_z(v)
                near = near + beside_rows(v, yh1[b, 0, c, pl.ds(x, 1)], yh1[b, 1, c, pl.ds(x, 1)])
                u[b, c, x + 1] = (1.0 - OMEGA) * v + (ld[b, c, x] + pull * near)
            return carry

        lax.fori_loop(k * step, (k + 1) * step, at_x, 0, unroll=2)

    def departure(b, k):
        return pltpu.make_async_copy(
            u.at[b, :, pl.ds(k * step + 1, step)], outs[b].at[:, pl.ds(k * step, step)], out_sem.at[b, k])

    for b in range(2):
        u[b, :, 0] = xh0[b, 0]
        u[b, :, nx + 1] = xh0[b, 1]
        w[b, :, 0] = xh1[b, 0]
        w[b, :, nx + 1] = xh1[b, 1]
        for copy in arrivals(b, 0):
            copy.wait()
        for k in range(chunks):
            if k + 1 < chunks:
                for copy in arrivals(b, k + 1):
                    copy.wait()
            first(b, k)
            if k >= 1:
                second(b, k - 1)
                departure(b, k - 1).start()
        second(b, chunks - 1)
        departure(b, chunks - 1).start()
    for b in range(2):
        for k in range(chunks):
            departure(b, k).wait()


def on_device(
    n_slab, n_sub,
    cav_disp, cav_load, cav_stiff, cav_clamp, mnt_disp, mnt_load, mnt_stiff, mnt_clamp,
    pair_owner, pair_row, pair_seg, pair_weight, pair_tilt, pair_gap,
):
    nx, ny, depth = cav_stiff.shape
    half = ny // 2
    dense = 3 * half
    targets = 2 * n_sub
    flat = lambda a: a.reshape(-1, depth)
    square = lambda a: a.reshape(-1, 128)
    x_shape = (2, 2, 3, ny, depth)
    y_shape = (2, 2, 3, nx, depth)
    hbm = pl.BlockSpec(memory_space=pl.ANY)
    vmem = pl.BlockSpec(memory_space=pltpu.VMEM)
    dma = pltpu.SemaphoreType.DMA
    shape = lambda dims: jax.ShapeDtypeStruct(dims, F32)
    rows = nx * ny
    halos = pl.pallas_call(
        functools.partial(contact_kernel, n_slab, n_sub, nx, ny),
        out_shape=[shape((2, dense, depth)), shape(x_shape), shape(y_shape), shape(x_shape), shape(y_shape)],
        in_specs=[hbm] * 8 + [vmem] * 6,
        out_specs=[vmem] * 5,
        scratch_shapes=[
            pltpu.VMEM((2, 3 * rows, depth), F32),
            pltpu.VMEM((2, 3 * rows, depth), F32),
            pltpu.VMEM((2, rows, depth), F32),
            pltpu.VMEM((2, rows, depth), jnp.int32),
            pltpu.VMEM((targets, dense, depth), F32),
            pltpu.VMEM((targets, dense, depth), F32),
            pltpu.VMEM((targets, dense, depth), F32),
            pltpu.VMEM(y_shape, F32),
            pltpu.VMEM(x_shape, F32),
            pltpu.VMEM(y_shape, F32),
            dma((targets,)), dma((targets,)), dma((targets,)), dma((targets,)),
            dma((2, 4)), dma((2, 4)), dma((2, 4)), dma((2, 4)), dma((8,)),
        ],
        compiler_params=pltpu.CompilerParams(
            collective_id=0, has_side_effects=True, vmem_limit_bytes=48 * 1024 * 1024),
        name="contact",
    )(
        flat(cav_disp), flat(mnt_disp), flat(cav_load), flat(mnt_load),
        flat(cav_stiff), flat(mnt_stiff), flat(cav_clamp), flat(mnt_clamp),
        square(pair_seg), square(pair_row), square(pair_owner), square(pair_weight), square(pair_gap), pair_tilt,
    )
    chunks = 8
    return tuple(pl.pallas_call(
        functools.partial(relax_kernel, nx, ny, chunks),
        out_shape=[shape(cav_disp.shape), shape(mnt_disp.shape)],
        in_specs=[hbm] * 8 + [vmem] * 5,
        out_specs=[hbm] * 2,
        scratch_shapes=[
            pltpu.VMEM((2, 3, nx + 2, ny, depth), F32),
            pltpu.VMEM((2, 3, nx + 2, ny, depth), F32),
            pltpu.VMEM((2, 3, nx, ny, depth), F32),
            pltpu.VMEM((2, nx, ny, depth), F32),
            pltpu.VMEM((2, nx, ny, depth), jnp.int32),
            dma((2, chunks, 4)), dma((2, chunks)),
        ],
        compiler_params=pltpu.CompilerParams(vmem_limit_bytes=48 * 1024 * 1024),
        name="relax",
    )(
        cav_disp, mnt_disp, cav_load, mnt_load, cav_stiff, mnt_stiff, cav_clamp, mnt_clamp, *halos
    ))


def solution(mesh):
    field = P(None, "slab", "sub", None)
    cells = P("slab", "sub", None)
    both = P(("slab", "sub"))
    return jax.shard_map(
        functools.partial(on_device, mesh.shape["slab"], mesh.shape["sub"]),
        mesh=mesh,
        in_specs=(
            field, field, cells, cells, field, field, cells, cells,
            P(("slab", "sub"), None), both, both, both, P(None, ("slab", "sub")), both,
        ),
        out_specs=(field, field),
        check_vma=False,
    )
```

```python
import functools
import jax
import jax.numpy as jnp
from jax import lax
from jax.experimental import pallas as pl
from jax.experimental.pallas import tpu as pltpu
from jax.sharding import PartitionSpec as P

OMEGA = 0.8
KCLAMP = 4.0
KNORM = 2.0
BETA = 4.0
MESH = pl.DeviceIdType.MESH
F32 = jnp.float32
BF16 = jnp.bfloat16
CHUNK = 256


def split3(v):
    hi = v.astype(BF16).astype(F32)
    rest = v - hi
    mid = rest.astype(BF16).astype(F32)
    return hi, mid, rest - mid


def beside_z(v):
    axis = v.ndim - 1
    depth = v.shape[axis]
    lane = lax.broadcasted_iota(jnp.int32, v.shape, axis)
    up = jnp.where(lane == 0, 0.0, pltpu.roll(v, 1, axis))
    down = jnp.where(lane == depth - 1, 0.0, pltpu.roll(v, depth - 1, axis))
    return up + down


def beside_rows(v, before, after):
    rows = v.shape[0]
    at = lax.broadcasted_iota(jnp.int32, v.shape, 0)
    up = jnp.where(at == 0, before, pltpu.roll(v, 1, 0))
    down = jnp.where(at == rows - 1, after, pltpu.roll(v, rows - 1, 0))
    return up + down


def coefficients(stiff, clamp):
    gain = OMEGA / (6.0 * stiff + KCLAMP * clamp.astype(F32))
    return gain, gain * stiff


def contact_kernel(
    n_slab, n_sub, nx, ny,
    disp_c, disp_m, load_c, load_m, stiff_c, stiff_m, clamp_c, clamp_m,
    seg_in, row_in, own_in, weight_in, gap0_in, tilt_in,
    react, xh0, yh0, xh1, yh1,
    seg, row, own, weight, gap0, tilt,
    u, ld, st, cl, tab, part, rec, yf, xs1, ys1,
    tab_s, tab_r, part_s, part_r, h0_s, h0_r, h1_s, h1_r, in_sem,
):
    s = lax.axis_index("slab")
    t = lax.axis_index("sub")
    depth = 128
    cells = nx * ny
    half = ny // 2
    dense = 3 * half
    pairs = seg.shape[0] * 128
    has_prev = s > 0
    has_next = s < n_slab - 1
    lane_of = (depth - 1, 0)

    loads = []
    for i, (src, dst) in enumerate((
        (disp_m, u.at[1]), (disp_c, u.at[0]),
        (seg_in, seg), (row_in, row), (own_in, own), (weight_in, weight), (gap0_in, gap0), (tilt_in, tilt),
        (stiff_m, st.at[1]), (clamp_m, cl.at[1]), (load_m, ld.at[1]),
        (stiff_c, st.at[0]), (clamp_c, cl.at[0]), (load_c, ld.at[0]),
    )):
        copy = pltpu.make_async_copy(src, dst, in_sem.at[i])
        copy.start()
        loads.append(copy)

    def peer(ds, d):
        return {"slab": s + ds, "sub": lax.rem(t + d, n_sub)}

    barrier = pltpu.get_barrier_semaphore()
    for d in range(1, n_sub):
        pl.semaphore_signal(barrier, inc=1, device_id=peer(0, d), device_id_type=MESH)

    @pl.when(has_prev)
    def _():
        for d in range(n_sub):
            pl.semaphore_signal(barrier, inc=1, device_id=peer(-1, d), device_id_type=MESH)

    @pl.when(has_next)
    def _():
        for d in range(n_sub):
            pl.semaphore_signal(barrier, inc=1, device_id=peer(1, d), device_id_type=MESH)

    def densify(b):
        zc = lane_of[b]
        lane = lax.broadcasted_iota(jnp.int32, (half, depth), 1)

        def at_x(x, acc):
            acc = list(acc)
            for c in range(3):
                for h in range(2):
                    want = x + nx * h
                    start = pl.multiple_of(c * cells + x * ny + half * h, 8)
                    tile = u[b, pl.ds(start, half), :]
                    moved = pltpu.roll(tile, lax.rem(want - zc + depth, depth), 1)
                    acc[c] = jnp.where(lane == want, moved, acc[c])
            return tuple(acc)

        zero = jnp.zeros((half, depth), F32)
        return jnp.concatenate(lax.fori_loop(0, nx, at_x, (zero,) * 3, unroll=4), axis=0)

    loads[0].wait()
    tab[t] = densify(1)
    for b, side in ((1, 0), (1, 1)):
        for c in range(3):
            yf[b, side, c] = u[b, pl.ds(c * cells + side * (ny - 1), nx, stride=ny), :]

    sides = has_prev.astype(jnp.int32) + has_next.astype(jnp.int32)
    pl.semaphore_wait(barrier, n_sub - 1 + n_sub * sides)

    def remote(src, dst, ss, rs, dev):
        return pltpu.make_async_remote_copy(
            src_ref=src, dst_ref=dst, send_sem=ss, recv_sem=rs, device_id=dev, device_id_type=MESH
        )

    def tab_copy(ds, d):
        k = d if ds == 0 else n_sub + d
        slot = t if ds == 0 else n_sub + t
        return remote(tab.at[t], tab.at[slot], tab_s.at[k], tab_r.at[slot], peer(ds, d))

    def tab_arrival(ds, d):
        slot = lax.rem(t + d, n_sub) + (n_sub if ds else 0)
        return remote(tab.at[t], tab.at[slot], tab_s.at[0], tab_r.at[slot], peer(ds, d))

    for d in range(1, n_sub):
        tab_copy(0, d).start()

    @pl.when(has_prev)
    def _():
        for d in range(n_sub):
            tab_copy(-1, d).start()

    @pl.when(jnp.logical_not(has_next))
    def _():
        tab[pl.ds(n_sub, n_sub)] = jnp.zeros((n_sub, dense, depth), F32)

    def ways():
        return (
            (0, has_prev, {"slab": s - 1, "sub": t}),
            (1, has_next, {"slab": s + 1, "sub": t}),
            (2, t > 0, {"slab": s, "sub": t - 1}),
            (3, t < n_sub - 1, {"slab": s, "sub": t + 1}),
        )

    def halo_copy(b, way, dev, xsrc, ysrc, xdst, ydst, ss, rs):
        other = way ^ 1
        if way < 2:
            src, dst = xsrc(b, way), xdst.at[b, other]
        else:
            src, dst = ysrc.at[b, way - 2], ydst.at[b, other - 2]
        return remote(src, dst, ss.at[b, way], rs.at[b, other], dev)

    def halo_arrival(b, way, dev, xdst, ydst, ss, rs):
        dst = xdst.at[b, way] if way < 2 else ydst.at[b, way - 2]
        return remote(dst, dst, ss.at[b, way], rs.at[b, way], dev)

    def x_plane(b, way):
        return u.at[b].reshape(3, nx, ny, depth).at[:, (nx - 1) * way]

    def start_halo0(b):
        for way, there, dev in ways():
            @pl.when(there)
            def _():
                halo_copy(b, way, dev, x_plane, yf, xh0, yh0, h0_s, h0_r).start()

            @pl.when(jnp.logical_not(there))
            def _():
                for out_x, out_y in ((xh0, yh0), (xh1, yh1)):
                    if way < 2:
                        out_x[b, way] = jnp.zeros((3, ny, depth), F32)
                    else:
                        out_y[b, way - 2] = jnp.zeros((3, nx, depth), F32)

    start_halo0(1)
    loads[1].wait()
    for side in range(2):
        for c in range(3):
            yf[0, side, c] = u[0, pl.ds(c * cells + side * (ny - 1), nx, stride=ny), :]
    start_halo0(0)
    cav_dense = densify(0)
    cav_parts = jnp.concatenate([v.astype(BF16) for v in split3(cav_dense)], axis=1)

    for d in range(1, n_sub):
        tab_arrival(0, d).wait_recv()

    @pl.when(has_next)
    def _():
        for d in range(n_sub):
            tab_arrival(1, d).wait_recv()

    for copy in loads[2:8]:
        copy.wait()
    targets = 2 * n_sub
    table = tab[...].reshape(targets * dense, depth)
    tab_parts = jnp.concatenate([v.astype(BF16) for v in split3(table)], axis=1)

    def line(ref, k):
        per = CHUNK // 128
        return jnp.concatenate([ref[k * per + i : k * per + i + 1, :] for i in range(per)], axis=1)

    dot = functools.partial(
        lax.dot_general, preferred_element_type=F32, precision=lax.Precision.DEFAULT
    )
    mnt_sum = jnp.zeros((targets * dense, depth), F32)
    cav_sum = jnp.zeros((dense, depth), F32)
    lane_id = lax.broadcasted_iota(jnp.int32, (depth, CHUNK), 0)
    key_id = lax.broadcasted_iota(jnp.int32, (targets * half, CHUNK), 0)
    small_id = lax.broadcasted_iota(jnp.int32, (half, CHUNK), 0)
    for k in range(pairs // CHUNK):
        def lanes(cell):
            return cell // ny + nx * (cell % ny // half)

        seg_k, row_k = line(seg, k), line(row, k)
        target = line(own, k) - s * n_sub
        hot_m = (lane_id == lanes(seg_k)).astype(F32).astype(BF16)
        hot_c = (lane_id == lanes(row_k)).astype(F32).astype(BF16)
        mask_m = key_id == target * half + seg_k % half
        mask_c = small_id == row_k % half
        rows_m = dot(tab_parts, jnp.concatenate([hot_m] * 3, axis=0), (((1,), (0,)), ((), ())))
        rows_c = dot(cav_parts, jnp.concatenate([hot_c] * 3, axis=0), (((1,), (0,)), ((), ())))
        sl_a = tilt[0:1, k * CHUNK : (k + 1) * CHUNK]
        sl_b = tilt[1:2, k * CHUNK : (k + 1) * CHUNK]
        scale = 1.0 / jnp.sqrt(1.0 + sl_a * sl_a + sl_b * sl_b)
        normal = (sl_a * scale, sl_b * scale, scale)
        gap = line(gap0, k)
        for c in range(3):
            mine = jnp.concatenate(
                [rows_m[o * dense + c * half : o * dense + (c + 1) * half] for o in range(targets)], axis=0
            )
            side_m = jnp.sum(jnp.where(mask_m, mine, 0.0), axis=0, keepdims=True)
            side_c = jnp.sum(
                jnp.where(mask_c, rows_c[c * half : (c + 1) * half], 0.0), axis=0, keepdims=True
            )
            gap = gap + normal[c] * (side_c - side_m)
        z = -BETA * gap
        soft = jnp.maximum(z, 0.0) + jnp.log1p(jnp.exp(-jnp.abs(z)))
        press = line(weight, k) * (KNORM * soft / BETA)
        push = [split3(press * normal[c]) for c in range(3)]
        left_m, left_c = [], []
        for p in range(3):
            left_m.append(jnp.concatenate(
                [
                    jnp.where(mask_m[o * half : (o + 1) * half], push[c][p], 0.0)
                    for o in range(targets) for c in range(3)
                ], axis=0).astype(BF16))
            left_c.append(jnp.concatenate(
                [jnp.where(mask_c, push[c][p], 0.0) for c in range(3)], axis=0).astype(BF16))
        mnt_sum = mnt_sum + dot(
            jnp.concatenate(left_m, axis=1), jnp.concatenate([hot_m] * 3, axis=1), (((1,), (1,)), ((), ())))
        cav_sum = cav_sum + dot(
            jnp.concatenate(left_c, axis=1), jnp.concatenate([hot_c] * 3, axis=1), (((1,), (1,)), ((), ())))
    part[...] = mnt_sum.reshape(targets, dense, depth)
    react[0] = cav_sum

    def part_copy(ds, d):
        k = d if ds == 0 else n_sub + d
        slot = t if ds == 0 else n_sub + t
        block = lax.rem(t + d, n_sub) + (n_sub if ds else 0)
        return remote(part.at[block], rec.at[slot], part_s.at[k], part_r.at[slot], peer(ds, d))

    def part_arrival(ds, d):
        slot = lax.rem(t + d, n_sub) + (n_sub if ds else 0)
        return remote(part.at[t], rec.at[slot], part_s.at[0], part_r.at[slot], peer(ds, d))

    @pl.when(has_next)
    def _():
        for d in range(n_sub):
            part_copy(1, d).start()

    for d in range(1, n_sub):
        part_copy(0, d).start()
    rec[t] = part[t]

    @pl.when(jnp.logical_not(has_prev))
    def _():
        rec[pl.ds(n_sub, n_sub)] = jnp.zeros((n_sub, dense, depth), F32)

    for copy in loads[8:]:
        copy.wait()
    for b in range(2):
        for way, there, dev in ways():
            @pl.when(there)
            def _():
                halo_arrival(b, way, dev, xh0, yh0, h0_s, h0_r).wait_recv()

    def faces(b):
        zc = lane_of[b]
        force_b = react[b]
        turned = jnp.transpose(jnp.concatenate(
            [force_b, jnp.zeros((depth - dense, depth), F32)], axis=0))
        for side in range(2):
            x0 = side * (nx - 1)
            at_x = pl.ds(x0 * ny, ny)
            gain, pull = coefficients(st[b, at_x, :], cl[b, at_x, :])
            lane = lax.broadcasted_iota(jnp.int32, (ny, depth), 1)
            for c in range(3):
                v = u[b, pl.ds(c * cells + x0 * ny, ny), :]
                inner = u[b, pl.ds(c * cells + (x0 + 1 - 2 * side) * ny, ny), :]
                near = xh0[b, side, c] + inner + beside_z(v)
                near = near + beside_rows(v, yh0[b, 0, c, x0 : x0 + 1], yh0[b, 1, c, x0 : x0 + 1])
                rows = force_b[c * half : (c + 1) * half]
                extra = jnp.concatenate(
                    [pltpu.roll(rows, (zc - x0 - nx * h) % depth, 1) for h in range(2)], axis=0)
                force = ld[b, pl.ds(c * cells + x0 * ny, ny), :] + jnp.where(lane == zc, extra, 0.0)
                xs1[b, side, c] = (1.0 - OMEGA) * v + (gain * force + pull * near)
            y0 = side * (ny - 1)
            at_y = pl.ds(y0, nx, stride=ny)
            gain, pull = coefficients(st[b, at_y, :], cl[b, at_y, :])
            lane = lax.broadcasted_iota(jnp.int32, (nx, depth), 1)
            for c in range(3):
                v = yf[b, side, c]
                inner = u[b, pl.ds(c * cells + y0 + 1 - 2 * side, nx, stride=ny), :]
                near = yh0[b, side, c] + inner + beside_z(v)
                near = near + beside_rows(v, xh0[b, 0, c, y0 : y0 + 1], xh0[b, 1, c, y0 : y0 + 1])
                rows = turned[nx * side : nx * side + nx]
                extra = pltpu.roll(rows, (zc - c * half - y0 % half) % depth, 1)
                force = ld[b, pl.ds(c * cells + y0, nx, stride=ny), :] + jnp.where(lane == zc, extra, 0.0)
                ys1[b, side, c] = (1.0 - OMEGA) * v + (gain * force + pull * near)
        for way, there, dev in ways():
            @pl.when(there)
            def _():
                halo_copy(b, way, dev, lambda b, w: xs1.at[b, w], ys1, xh1, yh1, h1_s, h1_r).start()

    faces(0)
    for d in range(1, n_sub):
        part_arrival(0, d).wait_recv()

    @pl.when(has_prev)
    def _():
        for d in range(n_sub):
            part_arrival(-1, d).wait_recv()

    total = rec[0]
    for o in range(1, targets):
        total = total + rec[o]
    react[1] = -total
    faces(1)

    for d in range(1, n_sub):
        tab_copy(0, d).wait_send()
        part_copy(0, d).wait_send()

    @pl.when(has_prev)
    def _():
        for d in range(n_sub):
            tab_copy(-1, d).wait_send()

    @pl.when(has_next)
    def _():
        for d in range(n_sub):
            part_copy(1, d).wait_send()

    for b in range(2):
        for way, there, dev in ways():
            @pl.when(there)
            def _():
                halo_copy(b, way, dev, x_plane, yf, xh0, yh0, h0_s, h0_r).wait_send()
                halo_copy(b, way, dev, lambda b, w: xs1.at[b, w], ys1, xh1, yh1, h1_s, h1_r).wait_send()
                halo_arrival(b, way, dev, xh1, yh1, h1_s, h1_r).wait_recv()


def relax_kernel(
    nx, ny, chunks,
    disp_c, disp_m, load_c, load_m, stiff_c, stiff_m, clamp_c, clamp_m,
    react, xh0, yh0, xh1, yh1,
    out_c, out_m,
    u, w, ld, st, cl, in_sem, out_sem,
):
    depth = 128
    half = ny // 2
    step = nx // chunks
    sources = ((disp_c, load_c, stiff_c, clamp_c), (disp_m, load_m, stiff_m, clamp_m))
    outs = (out_c, out_m)

    def arrivals(b, k):
        span = pl.ds(k * step, step)
        shifted = pl.ds(k * step + 1, step)
        disp, load, stiff, clamp = sources[b]
        return (
            pltpu.make_async_copy(disp.at[:, span], u.at[b, :, shifted], in_sem.at[b, k, 0]),
            pltpu.make_async_copy(load.at[:, span], ld.at[b, :, span], in_sem.at[b, k, 1]),
            pltpu.make_async_copy(stiff.at[span], st.at[b, span], in_sem.at[b, k, 2]),
            pltpu.make_async_copy(clamp.at[span], cl.at[b, span], in_sem.at[b, k, 3]),
        )

    for b in range(2):
        for k in range(chunks):
            for copy in arrivals(b, k):
                copy.start()

    lane = lax.broadcasted_iota(jnp.int32, (ny, depth), 1)

    def first(b, k):
        zc = (depth - 1, 0)[b]

        def at_x(x, carry):
            gain, pull = coefficients(st[b, x], cl[b, x])
            st[b, x] = pull
            for c in range(3):
                v = u[b, c, x + 1]
                near = u[b, c, x] + u[b, c, x + 2] + beside_z(v)
                near = near + beside_rows(v, yh0[b, 0, c, pl.ds(x, 1)], yh0[b, 1, c, pl.ds(x, 1)])
                rows = react[b, c * half : (c + 1) * half]
                extra = jnp.concatenate(
                    [pltpu.roll(rows, lax.rem(zc - x - nx * h + 2 * depth, depth), 1) for h in range(2)], axis=0)
                push = gain * (ld[b, c, x] + jnp.where(lane == zc, extra, 0.0))
                ld[b, c, x] = push
                w[b, c, x + 1] = (1.0 - OMEGA) * v + (push + pull * near)
            return carry

        lax.fori_loop(0, step, lambda i, carry: at_x(k * step + i, carry), 0, unroll=True)

    def second(b, k):
        def at_x(x, carry):
            pull = st[b, x]
            for c in range(3):
                v = w[b, c, x + 1]
                near = w[b, c, x] + w[b, c, x + 2] + beside_z(v)
                near = near + beside_rows(v, yh1[b, 0, c, pl.ds(x, 1)], yh1[b, 1, c, pl.ds(x, 1)])
                u[b, c, x + 1] = (1.0 - OMEGA) * v + (ld[b, c, x] + pull * near)
            return carry

        lax.fori_loop(0, step, lambda i, carry: at_x(k * step + i, carry), 0, unroll=True)

    def departure(b, k):
        return pltpu.make_async_copy(
            u.at[b, :, pl.ds(k * step + 1, step)], outs[b].at[:, pl.ds(k * step, step)], out_sem.at[b, k])

    for b in range(2):
        u[b, :, 0] = xh0[b, 0]
        u[b, :, nx + 1] = xh0[b, 1]
        w[b, :, 0] = xh1[b, 0]
        w[b, :, nx + 1] = xh1[b, 1]
        for copy in arrivals(b, 0):
            copy.wait()

        def chunk(k, carry, b=b):
            @pl.when(k + 1 < chunks)
            def _():
                for copy in arrivals(b, k + 1):
                    copy.wait()

            first(b, k)

            @pl.when(k >= 1)
            def _():
                second(b, k - 1)
                departure(b, k - 1).start()

            return carry

        lax.fori_loop(0, chunks, chunk, 0)
        second(b, chunks - 1)
        departure(b, chunks - 1).start()
    for b in range(2):
        for k in range(chunks):
            departure(b, k).wait()


def on_device(
    n_slab, n_sub,
    cav_disp, cav_load, cav_stiff, cav_clamp, mnt_disp, mnt_load, mnt_stiff, mnt_clamp,
    pair_owner, pair_row, pair_seg, pair_weight, pair_tilt, pair_gap,
):
    nx, ny, depth = cav_stiff.shape
    half = ny // 2
    dense = 3 * half
    targets = 2 * n_sub
    flat = lambda a: a.reshape(-1, depth)
    square = lambda a: a.reshape(-1, 128)
    x_shape = (2, 2, 3, ny, depth)
    y_shape = (2, 2, 3, nx, depth)
    hbm = pl.BlockSpec(memory_space=pltpu.HBM)
    vmem = pl.BlockSpec(memory_space=pltpu.VMEM)
    dma = pltpu.SemaphoreType.DMA
    shape = lambda dims: jax.ShapeDtypeStruct(dims, F32)
    rows = nx * ny
    pairs = pair_row.shape[0]
    halos = pl.pallas_call(
        functools.partial(contact_kernel, n_slab, n_sub, nx, ny),
        out_shape=[shape((2, dense, depth)), shape(x_shape), shape(y_shape), shape(x_shape), shape(y_shape)],
        in_specs=[hbm] * 14,
        out_specs=[vmem] * 5,
        scratch_shapes=[
            *[pltpu.VMEM((pairs // 128, 128), kind) for kind in (jnp.int32,) * 3 + (F32,) * 2],
            pltpu.VMEM((2, pairs), F32),
            pltpu.VMEM((2, 3 * rows, depth), F32),
            pltpu.VMEM((2, 3 * rows, depth), F32),
            pltpu.VMEM((2, rows, depth), F32),
            pltpu.VMEM((2, rows, depth), jnp.int32),
            pltpu.VMEM((targets, dense, depth), F32),
            pltpu.VMEM((targets, dense, depth), F32),
            pltpu.VMEM((targets, dense, depth), F32),
            pltpu.VMEM(y_shape, F32),
            pltpu.VMEM(x_shape, F32),
            pltpu.VMEM(y_shape, F32),
            dma((targets,)), dma((targets,)), dma((targets,)), dma((targets,)),
            dma((2, 4)), dma((2, 4)), dma((2, 4)), dma((2, 4)), dma((14,)),
        ],
        compiler_params=pltpu.CompilerParams(
            collective_id=0, has_side_effects=True, vmem_limit_bytes=65_500 * 1024),
        name="contact",
    )(
        flat(cav_disp), flat(mnt_disp), flat(cav_load), flat(mnt_load),
        flat(cav_stiff), flat(mnt_stiff), flat(cav_clamp), flat(mnt_clamp),
        square(pair_seg), square(pair_row), square(pair_owner), square(pair_weight), square(pair_gap), pair_tilt,
    )
    chunks = 8
    return tuple(pl.pallas_call(
        functools.partial(relax_kernel, nx, ny, chunks),
        out_shape=[shape(cav_disp.shape), shape(mnt_disp.shape)],
        in_specs=[hbm] * 8 + [vmem] * 5,
        out_specs=[hbm] * 2,
        scratch_shapes=[
            pltpu.VMEM((2, 3, nx + 2, ny, depth), F32),
            pltpu.VMEM((2, 3, nx + 2, ny, depth), F32),
            pltpu.VMEM((2, 3, nx, ny, depth), F32),
            pltpu.VMEM((2, nx, ny, depth), F32),
            pltpu.VMEM((2, nx, ny, depth), jnp.int32),
            dma((2, chunks, 4)), dma((2, chunks)),
        ],
        compiler_params=pltpu.CompilerParams(vmem_limit_bytes=65_500 * 1024),
        name="relax",
    )(
        cav_disp, mnt_disp, cav_load, mnt_load, cav_stiff, mnt_stiff, cav_clamp, mnt_clamp, *halos
    ))


def solution(mesh):
    field = P(None, "slab", "sub", None)
    cells = P("slab", "sub", None)
    both = P(("slab", "sub"))
    return jax.shard_map(
        functools.partial(on_device, mesh.shape["slab"], mesh.shape["sub"]),
        mesh=mesh,
        in_specs=(
            field, field, cells, cells, field, field, cells, cells,
            P(("slab", "sub"), None), both, both, both, P(None, ("slab", "sub")), both,
        ),
        out_specs=(field, field),
        check_vma=False,
    )
```

```python
import functools
import jax
import jax.numpy as jnp
from jax import lax
from jax.experimental import pallas as pl
from jax.experimental.pallas import tpu as pltpu
from jax.sharding import PartitionSpec as P

OMEGA = 0.8
KCLAMP = 4.0
KNORM = 2.0
BETA = 4.0
MESH = pl.DeviceIdType.MESH
F32 = jnp.float32
BF16 = jnp.bfloat16
CHUNK = 256
CHUNKS = 8


def split3(v):
    hi = v.astype(BF16).astype(F32)
    rest = v - hi
    mid = rest.astype(BF16).astype(F32)
    return hi, mid, rest - mid


def beside_z(v):
    axis = v.ndim - 1
    depth = v.shape[axis]
    lane = lax.broadcasted_iota(jnp.int32, v.shape, axis)
    up = jnp.where(lane == 0, 0.0, pltpu.roll(v, 1, axis))
    down = jnp.where(lane == depth - 1, 0.0, pltpu.roll(v, depth - 1, axis))
    return up + down


def beside_rows(v, before, after):
    rows = v.shape[0]
    at = lax.broadcasted_iota(jnp.int32, v.shape, 0)
    up = jnp.where(at == 0, before, pltpu.roll(v, 1, 0))
    down = jnp.where(at == rows - 1, after, pltpu.roll(v, rows - 1, 0))
    return up + down


def coefficients(stiff, clamp):
    gain = OMEGA / (6.0 * stiff + KCLAMP * clamp.astype(F32))
    return gain, gain * stiff


def contact_kernel(
    n_slab, n_sub, nx, ny,
    disp_c, disp_m, load_c, load_m, stiff_c, stiff_m, clamp_c, clamp_m,
    seg_in, row_in, own_in, weight_in, gap0_in, tilt_in,
    w_out, push_out, pull_out, xh1, yh1,
    react, xh0, yh0, w, seg, row, own, weight, gap0, tilt,
    u, ld, st, cl, tab, part, rec, yf, xs1, ys1,
    tab_s, tab_r, part_s, part_r, h0_s, h0_r, h1_s, h1_r, in_sem, out_sem,
):
    s = lax.axis_index("slab")
    t = lax.axis_index("sub")
    depth = 128
    cells = nx * ny
    half = ny // 2
    dense = 3 * half
    pairs = seg.shape[0] * 128
    has_prev = s > 0
    has_next = s < n_slab - 1
    lane_of = (depth - 1, 0)

    loads = []
    for i, (src, dst) in enumerate((
        (disp_m, u.at[1, :, pl.ds(ny, cells)]), (disp_c, u.at[0, :, pl.ds(ny, cells)]),
        (seg_in, seg), (row_in, row), (own_in, own), (weight_in, weight), (gap0_in, gap0), (tilt_in, tilt),
        (stiff_m, st.at[1]), (clamp_m, cl.at[1]), (load_m, ld.at[1]),
        (stiff_c, st.at[0]), (clamp_c, cl.at[0]), (load_c, ld.at[0]),
    )):
        copy = pltpu.make_async_copy(src, dst, in_sem.at[i])
        copy.start()
        loads.append(copy)

    def peer(ds, d):
        return {"slab": s + ds, "sub": lax.rem(t + d, n_sub)}

    barrier = pltpu.get_barrier_semaphore()
    for d in range(1, n_sub):
        pl.semaphore_signal(barrier, inc=1, device_id=peer(0, d), device_id_type=MESH)

    @pl.when(has_prev)
    def _():
        for d in range(n_sub):
            pl.semaphore_signal(barrier, inc=1, device_id=peer(-1, d), device_id_type=MESH)

    @pl.when(has_next)
    def _():
        for d in range(n_sub):
            pl.semaphore_signal(barrier, inc=1, device_id=peer(1, d), device_id_type=MESH)

    def densify(b):
        zc = lane_of[b]
        lane = lax.broadcasted_iota(jnp.int32, (half, depth), 1)

        def at_x(x, acc):
            acc = list(acc)
            for c in range(3):
                for h in range(2):
                    want = x + nx * h
                    start = pl.multiple_of(ny + x * ny + half * h, 8)
                    tile = u[b, c, pl.ds(start, half), :]
                    moved = pltpu.roll(tile, lax.rem(want - zc + depth, depth), 1)
                    acc[c] = jnp.where(lane == want, moved, acc[c])
            return tuple(acc)

        zero = jnp.zeros((half, depth), F32)
        return jnp.concatenate(lax.fori_loop(0, nx, at_x, (zero,) * 3, unroll=4), axis=0)

    loads[0].wait()
    tab[t] = densify(1)
    for b, side in ((1, 0), (1, 1)):
        for c in range(3):
            yf[b, side, c] = u[b, c, pl.ds(ny + side * (ny - 1), nx, stride=ny), :]

    sides = has_prev.astype(jnp.int32) + has_next.astype(jnp.int32)
    pl.semaphore_wait(barrier, n_sub - 1 + n_sub * sides)

    def remote(src, dst, ss, rs, dev):
        return pltpu.make_async_remote_copy(
            src_ref=src, dst_ref=dst, send_sem=ss, recv_sem=rs, device_id=dev, device_id_type=MESH
        )

    def tab_copy(ds, d):
        k = d if ds == 0 else n_sub + d
        slot = t if ds == 0 else n_sub + t
        return remote(tab.at[t], tab.at[slot], tab_s.at[k], tab_r.at[slot], peer(ds, d))

    def tab_arrival(ds, d):
        slot = lax.rem(t + d, n_sub) + (n_sub if ds else 0)
        return remote(tab.at[t], tab.at[slot], tab_s.at[0], tab_r.at[slot], peer(ds, d))

    for d in range(1, n_sub):
        tab_copy(0, d).start()

    @pl.when(has_prev)
    def _():
        for d in range(n_sub):
            tab_copy(-1, d).start()

    @pl.when(jnp.logical_not(has_next))
    def _():
        tab[pl.ds(n_sub, n_sub)] = jnp.zeros((n_sub, dense, depth), F32)

    def ways():
        return (
            (0, has_prev, {"slab": s - 1, "sub": t}),
            (1, has_next, {"slab": s + 1, "sub": t}),
            (2, t > 0, {"slab": s, "sub": t - 1}),
            (3, t < n_sub - 1, {"slab": s, "sub": t + 1}),
        )

    def halo_copy(b, way, dev, xsrc, ysrc, xdst, ydst, ss, rs):
        other = way ^ 1
        if way < 2:
            src, dst = xsrc(b, way), xdst.at[b, other]
        else:
            src, dst = ysrc.at[b, way - 2], ydst.at[b, other - 2]
        return remote(src, dst, ss.at[b, way], rs.at[b, other], dev)

    def halo_arrival(b, way, dev, xdst, ydst, ss, rs):
        dst = xdst.at[b, way] if way < 2 else ydst.at[b, way - 2]
        return remote(dst, dst, ss.at[b, way], rs.at[b, way], dev)

    def x_plane(b, way):
        return u.at[b, :, pl.ds(ny + (nx - 1) * ny * way, ny)]

    def start_halo0(b):
        for way, there, dev in ways():
            @pl.when(there)
            def _():
                halo_copy(b, way, dev, x_plane, yf, xh0, yh0, h0_s, h0_r).start()

            @pl.when(jnp.logical_not(there))
            def _():
                for out_x, out_y in ((xh0, yh0), (xh1, yh1)):
                    if way < 2:
                        out_x[b, way] = jnp.zeros((3, ny, depth), F32)
                    else:
                        out_y[b, way - 2] = jnp.zeros((3, nx, depth), F32)

    start_halo0(1)
    loads[1].wait()
    for side in range(2):
        for c in range(3):
            yf[0, side, c] = u[0, c, pl.ds(ny + side * (ny - 1), nx, stride=ny), :]
    start_halo0(0)
    cav_dense = densify(0)
    cav_parts = jnp.concatenate([v.astype(BF16) for v in split3(cav_dense)], axis=1)

    for d in range(1, n_sub):
        tab_arrival(0, d).wait_recv()

    @pl.when(has_next)
    def _():
        for d in range(n_sub):
            tab_arrival(1, d).wait_recv()

    for copy in loads[2:8]:
        copy.wait()
    targets = 2 * n_sub
    table = tab[...].reshape(targets * dense, depth)
    tab_parts = jnp.concatenate([v.astype(BF16) for v in split3(table)], axis=1)

    def line(ref, k):
        per = CHUNK // 128
        return jnp.concatenate([ref[k * per + i : k * per + i + 1, :] for i in range(per)], axis=1)

    dot = functools.partial(
        lax.dot_general, preferred_element_type=F32, precision=lax.Precision.DEFAULT
    )
    mnt_sum = jnp.zeros((targets * dense, depth), F32)
    cav_sum = jnp.zeros((dense, depth), F32)
    lane_id = lax.broadcasted_iota(jnp.int32, (depth, CHUNK), 0)
    key_id = lax.broadcasted_iota(jnp.int32, (targets * half, CHUNK), 0)
    small_id = lax.broadcasted_iota(jnp.int32, (half, CHUNK), 0)
    for k in range(pairs // CHUNK):
        def lanes(cell):
            return cell // ny + nx * (cell % ny // half)

        seg_k, row_k = line(seg, k), line(row, k)
        target = line(own, k) - s * n_sub
        hot_m = (lane_id == lanes(seg_k)).astype(F32).astype(BF16)
        hot_c = (lane_id == lanes(row_k)).astype(F32).astype(BF16)
        mask_m = key_id == target * half + seg_k % half
        mask_c = small_id == row_k % half
        rows_m = dot(tab_parts, jnp.concatenate([hot_m] * 3, axis=0), (((1,), (0,)), ((), ())))
        rows_c = dot(cav_parts, jnp.concatenate([hot_c] * 3, axis=0), (((1,), (0,)), ((), ())))
        sl_a = tilt[0:1, k * CHUNK : (k + 1) * CHUNK]
        sl_b = tilt[1:2, k * CHUNK : (k + 1) * CHUNK]
        scale = 1.0 / jnp.sqrt(1.0 + sl_a * sl_a + sl_b * sl_b)
        normal = (sl_a * scale, sl_b * scale, scale)
        gap = line(gap0, k)
        for c in range(3):
            mine = jnp.concatenate(
                [rows_m[o * dense + c * half : o * dense + (c + 1) * half] for o in range(targets)], axis=0
            )
            side_m = jnp.sum(jnp.where(mask_m, mine, 0.0), axis=0, keepdims=True)
            side_c = jnp.sum(
                jnp.where(mask_c, rows_c[c * half : (c + 1) * half], 0.0), axis=0, keepdims=True
            )
            gap = gap + normal[c] * (side_c - side_m)
        z = -BETA * gap
        soft = jnp.maximum(z, 0.0) + jnp.log1p(jnp.exp(-jnp.abs(z)))
        press = line(weight, k) * (KNORM * soft / BETA)
        push = [split3(press * normal[c]) for c in range(3)]
        left_m, left_c = [], []
        for p in range(3):
            left_m.append(jnp.concatenate(
                [
                    jnp.where(mask_m[o * half : (o + 1) * half], push[c][p], 0.0)
                    for o in range(targets) for c in range(3)
                ], axis=0).astype(BF16))
            left_c.append(jnp.concatenate(
                [jnp.where(mask_c, push[c][p], 0.0) for c in range(3)], axis=0).astype(BF16))
        mnt_sum = mnt_sum + dot(
            jnp.concatenate(left_m, axis=1), jnp.concatenate([hot_m] * 3, axis=1), (((1,), (1,)), ((), ())))
        cav_sum = cav_sum + dot(
            jnp.concatenate(left_c, axis=1), jnp.concatenate([hot_c] * 3, axis=1), (((1,), (1,)), ((), ())))
    part[...] = mnt_sum.reshape(targets, dense, depth)
    react[0] = cav_sum

    def part_copy(ds, d):
        k = d if ds == 0 else n_sub + d
        slot = t if ds == 0 else n_sub + t
        block = lax.rem(t + d, n_sub) + (n_sub if ds else 0)
        return remote(part.at[block], rec.at[slot], part_s.at[k], part_r.at[slot], peer(ds, d))

    def part_arrival(ds, d):
        slot = lax.rem(t + d, n_sub) + (n_sub if ds else 0)
        return remote(part.at[t], rec.at[slot], part_s.at[0], part_r.at[slot], peer(ds, d))

    @pl.when(has_next)
    def _():
        for d in range(n_sub):
            part_copy(1, d).start()

    for d in range(1, n_sub):
        part_copy(0, d).start()
    rec[t] = part[t]

    @pl.when(jnp.logical_not(has_prev))
    def _():
        rec[pl.ds(n_sub, n_sub)] = jnp.zeros((n_sub, dense, depth), F32)

    for copy in loads[8:]:
        copy.wait()
    for b in range(2):
        for way, there, dev in ways():
            @pl.when(there)
            def _():
                halo_arrival(b, way, dev, xh0, yh0, h0_s, h0_r).wait_recv()

    def faces(b):
        zc = lane_of[b]
        force_b = react[b]
        turned = jnp.transpose(jnp.concatenate(
            [force_b, jnp.zeros((depth - dense, depth), F32)], axis=0))
        for side in range(2):
            x0 = side * (nx - 1)
            at_x = pl.ds(x0 * ny, ny)
            gain, pull = coefficients(st[b, at_x, :], cl[b, at_x, :])
            lane = lax.broadcasted_iota(jnp.int32, (ny, depth), 1)
            for c in range(3):
                v = u[b, c, pl.ds(ny + x0 * ny, ny), :]
                inner = u[b, c, pl.ds(ny + (x0 + 1 - 2 * side) * ny, ny), :]
                near = xh0[b, side, c] + inner + beside_z(v)
                near = near + beside_rows(v, yh0[b, 0, c, x0 : x0 + 1], yh0[b, 1, c, x0 : x0 + 1])
                rows = force_b[c * half : (c + 1) * half]
                extra = jnp.concatenate(
                    [pltpu.roll(rows, (zc - x0 - nx * h) % depth, 1) for h in range(2)], axis=0)
                force = ld[b, c, pl.ds(x0 * ny, ny), :] + jnp.where(lane == zc, extra, 0.0)
                xs1[b, side, c] = (1.0 - OMEGA) * v + (gain * force + pull * near)
            y0 = side * (ny - 1)
            at_y = pl.ds(y0, nx, stride=ny)
            gain, pull = coefficients(st[b, at_y, :], cl[b, at_y, :])
            lane = lax.broadcasted_iota(jnp.int32, (nx, depth), 1)
            for c in range(3):
                v = yf[b, side, c]
                inner = u[b, c, pl.ds(ny + y0 + 1 - 2 * side, nx, stride=ny), :]
                near = yh0[b, side, c] + inner + beside_z(v)
                near = near + beside_rows(v, xh0[b, 0, c, y0 : y0 + 1], xh0[b, 1, c, y0 : y0 + 1])
                rows = turned[nx * side : nx * side + nx]
                extra = pltpu.roll(rows, (zc - c * half - y0 % half) % depth, 1)
                force = ld[b, c, pl.ds(y0, nx, stride=ny), :] + jnp.where(lane == zc, extra, 0.0)
                ys1[b, side, c] = (1.0 - OMEGA) * v + (gain * force + pull * near)
        for way, there, dev in ways():
            @pl.when(there)
            def _():
                halo_copy(b, way, dev, lambda b, w: xs1.at[b, w], ys1, xh1, yh1, h1_s, h1_r).start()

    planes = nx // CHUNKS
    zone = lax.broadcasted_iota(jnp.int32, (ny, depth), 1)

    def leaving(b, k):
        span = pl.ds(pl.multiple_of(k * planes * ny, 8), planes * ny)
        return (
            pltpu.make_async_copy(w.at[b, :, span], w_out.at[b, :, span], out_sem.at[b, k, 0]),
            pltpu.make_async_copy(ld.at[b, :, span], push_out.at[b, :, span], out_sem.at[b, k, 1]),
            pltpu.make_async_copy(st.at[b, span], pull_out.at[b, span], out_sem.at[b, k, 2]),
        )

    def first(b):
        zc = lane_of[b]
        u[b, :, pl.ds(0, ny)] = xh0[b, 0]
        u[b, :, pl.ds(ny + cells, ny)] = xh0[b, 1]

        def chunk(k, carry):
            for i in range(planes):
                x = k * planes + i
                at = [pl.ds(pl.multiple_of((x + j) * ny, 8), ny) for j in range(3)]
                gain, pull = coefficients(st[b, at[0], :], cl[b, at[0], :])
                st[b, at[0], :] = pull
                for c in range(3):
                    v = u[b, c, at[1], :]
                    near = u[b, c, at[0], :] + u[b, c, at[2], :] + beside_z(v)
                    near = near + beside_rows(v, yh0[b, 0, c, pl.ds(x, 1)], yh0[b, 1, c, pl.ds(x, 1)])
                    rows = react[b, c * half : (c + 1) * half]
                    extra = jnp.concatenate(
                        [pltpu.roll(rows, lax.rem(zc - x - nx * h + 2 * depth, depth), 1) for h in range(2)], axis=0)
                    push = gain * (ld[b, c, at[0], :] + jnp.where(zone == zc, extra, 0.0))
                    ld[b, c, at[0], :] = push
                    w[b, c, at[0], :] = (1.0 - OMEGA) * v + (push + pull * near)
            for copy in leaving(b, k):
                copy.start()
            return carry

        lax.fori_loop(0, CHUNKS, chunk, 0)

    faces(0)
    first(0)
    for d in range(1, n_sub):
        part_arrival(0, d).wait_recv()

    @pl.when(has_prev)
    def _():
        for d in range(n_sub):
            part_arrival(-1, d).wait_recv()

    total = rec[0]
    for o in range(1, targets):
        total = total + rec[o]
    react[1] = -total
    faces(1)
    first(1)

    for d in range(1, n_sub):
        tab_copy(0, d).wait_send()
        part_copy(0, d).wait_send()

    @pl.when(has_prev)
    def _():
        for d in range(n_sub):
            tab_copy(-1, d).wait_send()

    @pl.when(has_next)
    def _():
        for d in range(n_sub):
            part_copy(1, d).wait_send()

    for b in range(2):
        for way, there, dev in ways():
            @pl.when(there)
            def _():
                halo_copy(b, way, dev, x_plane, yf, xh0, yh0, h0_s, h0_r).wait_send()
                halo_copy(b, way, dev, lambda b, w: xs1.at[b, w], ys1, xh1, yh1, h1_s, h1_r).wait_send()
                halo_arrival(b, way, dev, xh1, yh1, h1_s, h1_r).wait_recv()
    for b in range(2):
        for k in range(CHUNKS):
            for copy in leaving(b, k):
                copy.wait()


def relax_kernel(
    nx, ny, w_in, push_in, pull_in, xh1, yh1, out_c, out_m, u, w, ld, st, in_sem, out_sem
):
    step = nx // CHUNKS
    outs = (out_c, out_m)

    def arrivals(b, k):
        span = pl.ds(k * step, step)
        return (
            pltpu.make_async_copy(w_in.at[b, :, span], w.at[b, :, pl.ds(k * step + 1, step)], in_sem.at[b, k, 0]),
            pltpu.make_async_copy(push_in.at[b, :, span], ld.at[b, :, span], in_sem.at[b, k, 1]),
            pltpu.make_async_copy(pull_in.at[b, span], st.at[b, span], in_sem.at[b, k, 2]),
        )

    def departure(b, k):
        span = pl.ds(k * step, step)
        return pltpu.make_async_copy(u.at[b, :, span], outs[b].at[:, span], out_sem.at[b, k])

    for b in range(2):
        for k in range(CHUNKS):
            for copy in arrivals(b, k):
                copy.start()

    for b in range(2):
        w[b, :, 0] = xh1[b, 0]
        w[b, :, nx + 1] = xh1[b, 1]
        for copy in arrivals(b, 0):
            copy.wait()

        def chunk(k, carry, b=b):
            @pl.when(k + 1 < CHUNKS)
            def _():
                for copy in arrivals(b, k + 1):
                    copy.wait()

            for i in range(step):
                x = k * step + i
                pull = st[b, x]
                for c in range(3):
                    v = w[b, c, x + 1]
                    near = w[b, c, x] + w[b, c, x + 2] + beside_z(v)
                    near = near + beside_rows(v, yh1[b, 0, c, pl.ds(x, 1)], yh1[b, 1, c, pl.ds(x, 1)])
                    u[b, c, x] = (1.0 - OMEGA) * v + (ld[b, c, x] + pull * near)
            departure(b, k).start()
            return carry

        lax.fori_loop(0, CHUNKS, chunk, 0)
    for b in range(2):
        for k in range(CHUNKS):
            departure(b, k).wait()


def on_device(
    n_slab, n_sub,
    cav_disp, cav_load, cav_stiff, cav_clamp, mnt_disp, mnt_load, mnt_stiff, mnt_clamp,
    pair_owner, pair_row, pair_seg, pair_weight, pair_tilt, pair_gap,
):
    nx, ny, depth = cav_stiff.shape
    half = ny // 2
    dense = 3 * half
    targets = 2 * n_sub
    flat = lambda a: a.reshape(*a.shape[:-3], -1, depth)
    square = lambda a: a.reshape(-1, 128)
    x_shape = (2, 2, 3, ny, depth)
    y_shape = (2, 2, 3, nx, depth)
    hbm = pl.BlockSpec(memory_space=pltpu.HBM)
    vmem = pl.BlockSpec(memory_space=pltpu.VMEM)
    dma = pltpu.SemaphoreType.DMA
    shape = lambda dims: jax.ShapeDtypeStruct(dims, F32)
    rows = nx * ny
    pairs = pair_row.shape[0]
    halos = pl.pallas_call(
        functools.partial(contact_kernel, n_slab, n_sub, nx, ny),
        out_shape=[
            shape((2, 3, rows, depth)), shape((2, 3, rows, depth)), shape((2, rows, depth)), shape(x_shape), shape(y_shape)],
        in_specs=[hbm] * 14,
        out_specs=[hbm] * 3 + [vmem] * 2,
        scratch_shapes=[
            pltpu.VMEM((2, dense, depth), F32), pltpu.VMEM(x_shape, F32), pltpu.VMEM(y_shape, F32),
            pltpu.VMEM((2, 3, rows, depth), F32),
            *[pltpu.VMEM((pairs // 128, 128), kind) for kind in (jnp.int32,) * 3 + (F32,) * 2],
            pltpu.VMEM((2, pairs), F32),
            pltpu.VMEM((2, 3, rows + 2 * ny, depth), F32),
            pltpu.VMEM((2, 3, rows, depth), F32),
            pltpu.VMEM((2, rows, depth), F32),
            pltpu.VMEM((2, rows, depth), jnp.int32),
            pltpu.VMEM((targets, dense, depth), F32),
            pltpu.VMEM((targets, dense, depth), F32),
            pltpu.VMEM((targets, dense, depth), F32),
            pltpu.VMEM(y_shape, F32),
            pltpu.VMEM(x_shape, F32),
            pltpu.VMEM(y_shape, F32),
            dma((targets,)), dma((targets,)), dma((targets,)), dma((targets,)),
            dma((2, 4)), dma((2, 4)), dma((2, 4)), dma((2, 4)), dma((14,)), dma((2, CHUNKS, 3)),
        ],
        compiler_params=pltpu.CompilerParams(
            collective_id=0, has_side_effects=True, vmem_limit_bytes=65_500 * 1024),
        name="contact",
    )(
        flat(cav_disp), flat(mnt_disp), flat(cav_load), flat(mnt_load),
        flat(cav_stiff), flat(mnt_stiff), flat(cav_clamp), flat(mnt_clamp),
        square(pair_seg), square(pair_row), square(pair_owner), square(pair_weight), square(pair_gap), pair_tilt,
    )
    w, push, pull, xh1, yh1 = halos
    solid = lambda a: a.reshape(*a.shape[:-2], nx, ny, depth)
    return tuple(pl.pallas_call(
        functools.partial(relax_kernel, nx, ny),
        out_shape=[shape(cav_disp.shape), shape(mnt_disp.shape)],
        in_specs=[hbm] * 3 + [vmem] * 2,
        out_specs=[hbm] * 2,
        scratch_shapes=[
            pltpu.VMEM((2, 3, nx, ny, depth), F32),
            pltpu.VMEM((2, 3, nx + 2, ny, depth), F32),
            pltpu.VMEM((2, 3, nx, ny, depth), F32),
            pltpu.VMEM((2, nx, ny, depth), F32),
            dma((2, CHUNKS, 3)), dma((2, CHUNKS)),
        ],
        compiler_params=pltpu.CompilerParams(vmem_limit_bytes=65_500 * 1024),
        name="relax",
    )(solid(w), solid(push), solid(pull), xh1, yh1))


def solution(mesh):
    field = P(None, "slab", "sub", None)
    cells = P("slab", "sub", None)
    both = P(("slab", "sub"))
    return jax.shard_map(
        functools.partial(on_device, mesh.shape["slab"], mesh.shape["sub"]),
        mesh=mesh,
        in_specs=(
            field, field, cells, cells, field, field, cells, cells,
            P(("slab", "sub"), None), both, both, both, P(None, ("slab", "sub")), both,
        ),
        out_specs=(field, field),
        check_vma=False,
    )
```

```python
import functools
import jax
import jax.numpy as jnp
from jax import lax
from jax.experimental import pallas as pl
from jax.experimental.pallas import tpu as pltpu
from jax.sharding import PartitionSpec as P

OMEGA = 0.8
KCLAMP = 4.0
KNORM = 2.0
BETA = 4.0
MESH = pl.DeviceIdType.MESH
F32 = jnp.float32
BF16 = jnp.bfloat16
CHUNK = 256
CHUNKS = 8


def split2(v):
    hi = v.astype(BF16).astype(F32)
    return hi, v - hi


def beside_z(v):
    axis = v.ndim - 1
    depth = v.shape[axis]
    lane = lax.broadcasted_iota(jnp.int32, v.shape, axis)
    up = jnp.where(lane == 0, 0.0, pltpu.roll(v, 1, axis))
    down = jnp.where(lane == depth - 1, 0.0, pltpu.roll(v, depth - 1, axis))
    return up + down


def beside_rows(v, before, after):
    rows = v.shape[0]
    at = lax.broadcasted_iota(jnp.int32, v.shape, 0)
    up = jnp.where(at == 0, before, pltpu.roll(v, 1, 0))
    down = jnp.where(at == rows - 1, after, pltpu.roll(v, rows - 1, 0))
    return up + down


def coefficients(stiff, clamp):
    gain = OMEGA / (6.0 * stiff + KCLAMP * clamp.astype(F32))
    return gain, gain * stiff


def contact_kernel(
    n_slab, n_sub, nx, ny,
    disp_c, disp_m, load_c, load_m, stiff_c, stiff_m, clamp_c, clamp_m,
    seg_in, row_in, own_in, weight_in, gap0_in, tilt_in,
    w_out, push_out, pull_out, xh1, yh1,
    react, xh0, yh0, w, seg, row, own, weight, gap0, tilt,
    u, ld, st, cl, tab, part, rec, yf, xs1, ys1,
    tab_s, tab_r, part_s, part_r, h0_s, h0_r, h1_s, h1_r, in_sem, out_sem,
):
    s = lax.axis_index("slab")
    t = lax.axis_index("sub")
    depth = 128
    cells = nx * ny
    half = ny // 2
    dense = 3 * half
    pairs = seg.shape[0] * 128
    has_prev = s > 0
    has_next = s < n_slab - 1
    lane_of = (depth - 1, 0)

    def peer(ds, d):
        return {"slab": s + ds, "sub": lax.rem(t + d, n_sub)}

    barrier = pltpu.get_barrier_semaphore()
    for d in range(1, n_sub):
        pl.semaphore_signal(barrier, inc=1, device_id=peer(0, d), device_id_type=MESH)

    @pl.when(has_prev)
    def _():
        for d in range(n_sub):
            pl.semaphore_signal(barrier, inc=1, device_id=peer(-1, d), device_id_type=MESH)

    @pl.when(has_next)
    def _():
        for d in range(n_sub):
            pl.semaphore_signal(barrier, inc=1, device_id=peer(1, d), device_id_type=MESH)

    loads = []
    for i, (src, dst) in enumerate((
        (disp_m, u.at[1, :, pl.ds(ny, cells)]), (disp_c, u.at[0, :, pl.ds(ny, cells)]),
        (seg_in, seg), (row_in, row), (own_in, own), (weight_in, weight), (gap0_in, gap0), (tilt_in, tilt),
        (stiff_m, st.at[1]), (clamp_m, cl.at[1]), (load_m, ld.at[1]),
        (stiff_c, st.at[0]), (clamp_c, cl.at[0]), (load_c, ld.at[0]),
    )):
        copy = pltpu.make_async_copy(src, dst, in_sem.at[i])
        copy.start()
        loads.append(copy)

    def densify(b):
        zc = lane_of[b]
        lane = lax.broadcasted_iota(jnp.int32, (half, depth), 1)

        def at_x(x, acc):
            acc = list(acc)
            for c in range(3):
                for h in range(2):
                    want = x + nx * h
                    start = pl.multiple_of(ny + x * ny + half * h, 8)
                    tile = u[b, c, pl.ds(start, half), :]
                    moved = pltpu.roll(tile, lax.rem(want - zc + depth, depth), 1)
                    acc[c] = jnp.where(lane == want, moved, acc[c])
            return tuple(acc)

        zero = jnp.zeros((half, depth), F32)
        return jnp.concatenate(lax.fori_loop(0, nx, at_x, (zero,) * 3, unroll=8), axis=0)

    loads[0].wait()
    tab[t] = densify(1)
    for b, side in ((1, 0), (1, 1)):
        for c in range(3):
            yf[b, side, c] = u[b, c, pl.ds(ny + side * (ny - 1), nx, stride=ny), :]

    sides = has_prev.astype(jnp.int32) + has_next.astype(jnp.int32)
    pl.semaphore_wait(barrier, n_sub - 1 + n_sub * sides)

    def remote(src, dst, ss, rs, dev):
        return pltpu.make_async_remote_copy(
            src_ref=src, dst_ref=dst, send_sem=ss, recv_sem=rs, device_id=dev, device_id_type=MESH
        )

    def tab_copy(ds, d):
        k = d if ds == 0 else n_sub + d
        slot = t if ds == 0 else n_sub + t
        return remote(tab.at[t], tab.at[slot], tab_s.at[k], tab_r.at[slot], peer(ds, d))

    def tab_arrival(ds, d):
        slot = lax.rem(t + d, n_sub) + (n_sub if ds else 0)
        return remote(tab.at[t], tab.at[slot], tab_s.at[0], tab_r.at[slot], peer(ds, d))

    for d in range(1, n_sub):
        tab_copy(0, d).start()

    @pl.when(has_prev)
    def _():
        for d in range(n_sub):
            tab_copy(-1, d).start()

    @pl.when(jnp.logical_not(has_next))
    def _():
        tab[pl.ds(n_sub, n_sub)] = jnp.zeros((n_sub, dense, depth), F32)

    def ways():
        return (
            (0, has_prev, {"slab": s - 1, "sub": t}),
            (1, has_next, {"slab": s + 1, "sub": t}),
            (2, t > 0, {"slab": s, "sub": t - 1}),
            (3, t < n_sub - 1, {"slab": s, "sub": t + 1}),
        )

    def halo_copy(b, way, dev, xsrc, ysrc, xdst, ydst, ss, rs):
        other = way ^ 1
        if way < 2:
            src, dst = xsrc(b, way), xdst.at[b, other]
        else:
            src, dst = ysrc.at[b, way - 2], ydst.at[b, other - 2]
        return remote(src, dst, ss.at[b, way], rs.at[b, other], dev)

    def halo_arrival(b, way, dev, xdst, ydst, ss, rs):
        dst = xdst.at[b, way] if way < 2 else ydst.at[b, way - 2]
        return remote(dst, dst, ss.at[b, way], rs.at[b, way], dev)

    def x_plane(b, way):
        return u.at[b, :, pl.ds(ny + (nx - 1) * ny * way, ny)]

    def start_halo0(b):
        for way, there, dev in ways():
            @pl.when(there)
            def _():
                halo_copy(b, way, dev, x_plane, yf, xh0, yh0, h0_s, h0_r).start()

            @pl.when(jnp.logical_not(there))
            def _():
                for out_x, out_y in ((xh0, yh0), (xh1, yh1)):
                    if way < 2:
                        out_x[b, way] = jnp.zeros((3, ny, depth), F32)
                    else:
                        out_y[b, way - 2] = jnp.zeros((3, nx, depth), F32)

    start_halo0(1)
    loads[1].wait()
    for side in range(2):
        for c in range(3):
            yf[0, side, c] = u[0, c, pl.ds(ny + side * (ny - 1), nx, stride=ny), :]
    start_halo0(0)
    cav_dense = densify(0)
    cav_parts = jnp.concatenate([v.astype(BF16) for v in split2(cav_dense)], axis=1)

    for d in range(1, n_sub):
        tab_arrival(0, d).wait_recv()

    @pl.when(has_next)
    def _():
        for d in range(n_sub):
            tab_arrival(1, d).wait_recv()

    for copy in loads[2:8]:
        copy.wait()
    targets = 2 * n_sub
    table = tab[...].reshape(targets * dense, depth)
    tab_parts = jnp.concatenate([v.astype(BF16) for v in split2(table)], axis=1)

    def line(ref, k):
        per = CHUNK // 128
        return jnp.concatenate([ref[k * per + i : k * per + i + 1, :] for i in range(per)], axis=1)

    dot = functools.partial(
        lax.dot_general, preferred_element_type=F32, precision=lax.Precision.DEFAULT
    )
    mnt_sum = jnp.zeros((targets * dense, depth), F32)
    cav_sum = jnp.zeros((dense, depth), F32)
    lane_id = lax.broadcasted_iota(jnp.int32, (depth, CHUNK), 0)
    key_id = lax.broadcasted_iota(jnp.int32, (targets * half, CHUNK), 0)
    small_id = lax.broadcasted_iota(jnp.int32, (half, CHUNK), 0)
    for k in range(pairs // CHUNK):
        def lanes(cell):
            return cell // ny + nx * (cell % ny // half)

        seg_k, row_k = line(seg, k), line(row, k)
        target = line(own, k) - s * n_sub
        hot_m = (lane_id == lanes(seg_k)).astype(F32).astype(BF16)
        hot_c = (lane_id == lanes(row_k)).astype(F32).astype(BF16)
        mask_m = key_id == target * half + seg_k % half
        mask_c = small_id == row_k % half
        rows_m = dot(tab_parts, jnp.concatenate([hot_m] * 2, axis=0), (((1,), (0,)), ((), ())))
        rows_c = dot(cav_parts, jnp.concatenate([hot_c] * 2, axis=0), (((1,), (0,)), ((), ())))
        sl_a = tilt[0:1, k * CHUNK : (k + 1) * CHUNK]
        sl_b = tilt[1:2, k * CHUNK : (k + 1) * CHUNK]
        scale = 1.0 / jnp.sqrt(1.0 + sl_a * sl_a + sl_b * sl_b)
        normal = (sl_a * scale, sl_b * scale, scale)
        gap = line(gap0, k)
        for c in range(3):
            mine = jnp.concatenate(
                [rows_m[o * dense + c * half : o * dense + (c + 1) * half] for o in range(targets)], axis=0
            )
            side_m = jnp.sum(jnp.where(mask_m, mine, 0.0), axis=0, keepdims=True)
            side_c = jnp.sum(
                jnp.where(mask_c, rows_c[c * half : (c + 1) * half], 0.0), axis=0, keepdims=True
            )
            gap = gap + normal[c] * (side_c - side_m)
        z = -BETA * gap
        soft = jnp.maximum(z, 0.0) + jnp.log1p(jnp.exp(-jnp.abs(z)))
        press = line(weight, k) * (KNORM * soft / BETA)
        push = [split2(press * normal[c]) for c in range(3)]
        left_m, left_c = [], []
        for p in range(2):
            left_m.append(jnp.concatenate(
                [
                    jnp.where(mask_m[o * half : (o + 1) * half], push[c][p], 0.0)
                    for o in range(targets) for c in range(3)
                ], axis=0).astype(BF16))
            left_c.append(jnp.concatenate(
                [jnp.where(mask_c, push[c][p], 0.0) for c in range(3)], axis=0).astype(BF16))
        mnt_sum = mnt_sum + dot(
            jnp.concatenate(left_m, axis=1), jnp.concatenate([hot_m] * 2, axis=1), (((1,), (1,)), ((), ())))
        cav_sum = cav_sum + dot(
            jnp.concatenate(left_c, axis=1), jnp.concatenate([hot_c] * 2, axis=1), (((1,), (1,)), ((), ())))
    part[...] = mnt_sum.reshape(targets, dense, depth)
    react[0] = cav_sum

    def part_copy(ds, d):
        k = d if ds == 0 else n_sub + d
        slot = t if ds == 0 else n_sub + t
        block = lax.rem(t + d, n_sub) + (n_sub if ds else 0)
        return remote(part.at[block], rec.at[slot], part_s.at[k], part_r.at[slot], peer(ds, d))

    def part_arrival(ds, d):
        slot = lax.rem(t + d, n_sub) + (n_sub if ds else 0)
        return remote(part.at[t], rec.at[slot], part_s.at[0], part_r.at[slot], peer(ds, d))

    @pl.when(has_next)
    def _():
        for d in range(n_sub):
            part_copy(1, d).start()

    for d in range(1, n_sub):
        part_copy(0, d).start()
    rec[t] = part[t]

    @pl.when(jnp.logical_not(has_prev))
    def _():
        rec[pl.ds(n_sub, n_sub)] = jnp.zeros((n_sub, dense, depth), F32)

    for copy in loads[8:]:
        copy.wait()
    for b in range(2):
        for way, there, dev in ways():
            @pl.when(there)
            def _():
                halo_arrival(b, way, dev, xh0, yh0, h0_s, h0_r).wait_recv()

    def faces(b):
        zc = lane_of[b]
        force_b = react[b]
        turned = jnp.transpose(jnp.concatenate(
            [force_b, jnp.zeros((depth - dense, depth), F32)], axis=0))
        for side in range(2):
            x0 = side * (nx - 1)
            at_x = pl.ds(x0 * ny, ny)
            gain, pull = coefficients(st[b, at_x, :], cl[b, at_x, :])
            lane = lax.broadcasted_iota(jnp.int32, (ny, depth), 1)
            for c in range(3):
                v = u[b, c, pl.ds(ny + x0 * ny, ny), :]
                inner = u[b, c, pl.ds(ny + (x0 + 1 - 2 * side) * ny, ny), :]
                near = xh0[b, side, c] + inner + beside_z(v)
                near = near + beside_rows(v, yh0[b, 0, c, x0 : x0 + 1], yh0[b, 1, c, x0 : x0 + 1])
                rows = force_b[c * half : (c + 1) * half]
                extra = jnp.concatenate(
                    [pltpu.roll(rows, (zc - x0 - nx * h) % depth, 1) for h in range(2)], axis=0)
                force = ld[b, c, pl.ds(x0 * ny, ny), :] + jnp.where(lane == zc, extra, 0.0)
                xs1[b, side, c] = (1.0 - OMEGA) * v + (gain * force + pull * near)
            y0 = side * (ny - 1)
            at_y = pl.ds(y0, nx, stride=ny)
            gain, pull = coefficients(st[b, at_y, :], cl[b, at_y, :])
            lane = lax.broadcasted_iota(jnp.int32, (nx, depth), 1)
            for c in range(3):
                v = yf[b, side, c]
                inner = u[b, c, pl.ds(ny + y0 + 1 - 2 * side, nx, stride=ny), :]
                near = yh0[b, side, c] + inner + beside_z(v)
                near = near + beside_rows(v, xh0[b, 0, c, y0 : y0 + 1], xh0[b, 1, c, y0 : y0 + 1])
                rows = turned[nx * side : nx * side + nx]
                extra = pltpu.roll(rows, (zc - c * half - y0 % half) % depth, 1)
                force = ld[b, c, pl.ds(y0, nx, stride=ny), :] + jnp.where(lane == zc, extra, 0.0)
                ys1[b, side, c] = (1.0 - OMEGA) * v + (gain * force + pull * near)
        for way, there, dev in ways():
            @pl.when(there)
            def _():
                halo_copy(b, way, dev, lambda b, w: xs1.at[b, w], ys1, xh1, yh1, h1_s, h1_r).start()

    planes = nx // CHUNKS
    zone = lax.broadcasted_iota(jnp.int32, (ny, depth), 1)

    def leaving(b, k):
        span = pl.ds(pl.multiple_of(k * planes * ny, 8), planes * ny)
        return (
            pltpu.make_async_copy(w.at[b, :, span], w_out.at[b, :, span], out_sem.at[b, k, 0]),
            pltpu.make_async_copy(ld.at[b, :, span], push_out.at[b, :, span], out_sem.at[b, k, 1]),
            pltpu.make_async_copy(st.at[b, span], pull_out.at[b, span], out_sem.at[b, k, 2]),
        )

    def first(b):
        zc = lane_of[b]
        u[b, :, pl.ds(0, ny)] = xh0[b, 0]
        u[b, :, pl.ds(ny + cells, ny)] = xh0[b, 1]

        def chunk(k, carry):
            for i in range(planes):
                x = k * planes + i
                at = [pl.ds(pl.multiple_of((x + j) * ny, 8), ny) for j in range(3)]
                gain, pull = coefficients(st[b, at[0], :], cl[b, at[0], :])
                st[b, at[0], :] = pull
                for c in range(3):
                    v = u[b, c, at[1], :]
                    near = u[b, c, at[0], :] + u[b, c, at[2], :] + beside_z(v)
                    near = near + beside_rows(v, yh0[b, 0, c, pl.ds(x, 1)], yh0[b, 1, c, pl.ds(x, 1)])
                    rows = react[b, c * half : (c + 1) * half]
                    extra = jnp.concatenate(
                        [pltpu.roll(rows, lax.rem(zc - x - nx * h + 2 * depth, depth), 1) for h in range(2)], axis=0)
                    push = gain * (ld[b, c, at[0], :] + jnp.where(zone == zc, extra, 0.0))
                    ld[b, c, at[0], :] = push
                    w[b, c, at[0], :] = (1.0 - OMEGA) * v + (push + pull * near)
            for copy in leaving(b, k):
                copy.start()
            return carry

        lax.fori_loop(0, CHUNKS, chunk, 0)

    faces(0)
    first(0)
    for d in range(1, n_sub):
        part_arrival(0, d).wait_recv()

    @pl.when(has_prev)
    def _():
        for d in range(n_sub):
            part_arrival(-1, d).wait_recv()

    total = rec[0]
    for o in range(1, targets):
        total = total + rec[o]
    react[1] = -total
    faces(1)
    first(1)

    for d in range(1, n_sub):
        tab_copy(0, d).wait_send()
        part_copy(0, d).wait_send()

    @pl.when(has_prev)
    def _():
        for d in range(n_sub):
            tab_copy(-1, d).wait_send()

    @pl.when(has_next)
    def _():
        for d in range(n_sub):
            part_copy(1, d).wait_send()

    for b in range(2):
        for way, there, dev in ways():
            @pl.when(there)
            def _():
                halo_copy(b, way, dev, x_plane, yf, xh0, yh0, h0_s, h0_r).wait_send()
                halo_copy(b, way, dev, lambda b, w: xs1.at[b, w], ys1, xh1, yh1, h1_s, h1_r).wait_send()
                halo_arrival(b, way, dev, xh1, yh1, h1_s, h1_r).wait_recv()
    for b in range(2):
        for k in range(CHUNKS):
            for copy in leaving(b, k):
                copy.wait()


def relax_kernel(
    nx, ny, w_in, push_in, pull_in, xh1, yh1, out_c, out_m, u, w, ld, st, in_sem, out_sem
):
    step = nx // CHUNKS
    outs = (out_c, out_m)

    def arrivals(b, k):
        span = pl.ds(k * step, step)
        return (
            pltpu.make_async_copy(w_in.at[b, :, span], w.at[b, :, pl.ds(k * step + 1, step)], in_sem.at[b, k, 0]),
            pltpu.make_async_copy(push_in.at[b, :, span], ld.at[b, :, span], in_sem.at[b, k, 1]),
            pltpu.make_async_copy(pull_in.at[b, span], st.at[b, span], in_sem.at[b, k, 2]),
        )

    def departure(b, k):
        span = pl.ds(k * step, step)
        return pltpu.make_async_copy(u.at[b, :, span], outs[b].at[:, span], out_sem.at[b, k])

    for b in range(2):
        for k in range(CHUNKS):
            for copy in arrivals(b, k):
                copy.start()

    for b in range(2):
        w[b, :, 0] = xh1[b, 0]
        w[b, :, nx + 1] = xh1[b, 1]
        for copy in arrivals(b, 0):
            copy.wait()

        def chunk(k, carry, b=b):
            @pl.when(k + 1 < CHUNKS)
            def _():
                for copy in arrivals(b, k + 1):
                    copy.wait()

            for i in range(step):
                x = k * step + i
                pull = st[b, x]
                for c in range(3):
                    v = w[b, c, x + 1]
                    near = w[b, c, x] + w[b, c, x + 2] + beside_z(v)
                    near = near + beside_rows(v, yh1[b, 0, c, pl.ds(x, 1)], yh1[b, 1, c, pl.ds(x, 1)])
                    u[b, c, x] = (1.0 - OMEGA) * v + (ld[b, c, x] + pull * near)
            departure(b, k).start()
            return carry

        lax.fori_loop(0, CHUNKS, chunk, 0)
    for b in range(2):
        for k in range(CHUNKS):
            departure(b, k).wait()


def on_device(
    n_slab, n_sub,
    cav_disp, cav_load, cav_stiff, cav_clamp, mnt_disp, mnt_load, mnt_stiff, mnt_clamp,
    pair_owner, pair_row, pair_seg, pair_weight, pair_tilt, pair_gap,
):
    nx, ny, depth = cav_stiff.shape
    half = ny // 2
    dense = 3 * half
    targets = 2 * n_sub
    flat = lambda a: a.reshape(*a.shape[:-3], -1, depth)
    square = lambda a: a.reshape(-1, 128)
    x_shape = (2, 2, 3, ny, depth)
    y_shape = (2, 2, 3, nx, depth)
    hbm = pl.BlockSpec(memory_space=pltpu.HBM)
    vmem = pl.BlockSpec(memory_space=pltpu.VMEM)
    dma = pltpu.SemaphoreType.DMA
    shape = lambda dims: jax.ShapeDtypeStruct(dims, F32)
    rows = nx * ny
    pairs = pair_row.shape[0]
    halos = pl.pallas_call(
        functools.partial(contact_kernel, n_slab, n_sub, nx, ny),
        out_shape=[
            shape((2, 3, rows, depth)), shape((2, 3, rows, depth)), shape((2, rows, depth)), shape(x_shape), shape(y_shape)],
        in_specs=[hbm] * 14,
        out_specs=[hbm] * 3 + [vmem] * 2,
        scratch_shapes=[
            pltpu.VMEM((2, dense, depth), F32), pltpu.VMEM(x_shape, F32), pltpu.VMEM(y_shape, F32),
            pltpu.VMEM((2, 3, rows, depth), F32),
            *[pltpu.VMEM((pairs // 128, 128), kind) for kind in (jnp.int32,) * 3 + (F32,) * 2],
            pltpu.VMEM((2, pairs), F32),
            pltpu.VMEM((2, 3, rows + 2 * ny, depth), F32),
            pltpu.VMEM((2, 3, rows, depth), F32),
            pltpu.VMEM((2, rows, depth), F32),
            pltpu.VMEM((2, rows, depth), jnp.int32),
            pltpu.VMEM((targets, dense, depth), F32),
            pltpu.VMEM((targets, dense, depth), F32),
            pltpu.VMEM((targets, dense, depth), F32),
            pltpu.VMEM(y_shape, F32),
            pltpu.VMEM(x_shape, F32),
            pltpu.VMEM(y_shape, F32),
            dma((targets,)), dma((targets,)), dma((targets,)), dma((targets,)),
            dma((2, 4)), dma((2, 4)), dma((2, 4)), dma((2, 4)), dma((14,)), dma((2, CHUNKS, 3)),
        ],
        compiler_params=pltpu.CompilerParams(
            collective_id=0, has_side_effects=True, vmem_limit_bytes=65_500 * 1024),
        name="contact",
    )(
        flat(cav_disp), flat(mnt_disp), flat(cav_load), flat(mnt_load),
        flat(cav_stiff), flat(mnt_stiff), flat(cav_clamp), flat(mnt_clamp),
        square(pair_seg), square(pair_row), square(pair_owner), square(pair_weight), square(pair_gap), pair_tilt,
    )
    w, push, pull, xh1, yh1 = halos
    solid = lambda a: a.reshape(*a.shape[:-2], nx, ny, depth)
    return tuple(pl.pallas_call(
        functools.partial(relax_kernel, nx, ny),
        out_shape=[shape(cav_disp.shape), shape(mnt_disp.shape)],
        in_specs=[hbm] * 3 + [vmem] * 2,
        out_specs=[hbm] * 2,
        scratch_shapes=[
            pltpu.VMEM((2, 3, nx, ny, depth), F32),
            pltpu.VMEM((2, 3, nx + 2, ny, depth), F32),
            pltpu.VMEM((2, 3, nx, ny, depth), F32),
            pltpu.VMEM((2, nx, ny, depth), F32),
            dma((2, CHUNKS, 3)), dma((2, CHUNKS)),
        ],
        compiler_params=pltpu.CompilerParams(vmem_limit_bytes=65_500 * 1024),
        name="relax",
    )(solid(w), solid(push), solid(pull), xh1, yh1))


def solution(mesh):
    field = P(None, "slab", "sub", None)
    cells = P("slab", "sub", None)
    both = P(("slab", "sub"))
    return jax.shard_map(
        functools.partial(on_device, mesh.shape["slab"], mesh.shape["sub"]),
        mesh=mesh,
        in_specs=(
            field, field, cells, cells, field, field, cells, cells,
            P(("slab", "sub"), None), both, both, both, P(None, ("slab", "sub")), both,
        ),
        out_specs=(field, field),
        check_vma=False,
    )
```
